512 devices in a mesh: patch: 64 (over y, z_hi, x), tensor: 8 (over z_lo, core).
Axes of the slice: x: 4, y: 4, z: 16 (z_hi: 4, z_lo: 4; z = z_hi * 4 + z_lo), core: 2. Of those that a mesh axis runs over, the one named last changes fastest.
Arguments:
- fresh_qkv: bfloat16 [3, 8192, 3072], P(None, 'patch', 'tensor'), may hold values from -14 to 14
- stale_kv: bfloat16 [2, 8192, 3072], P(None, 'patch', 'tensor'), may hold values from -6 to 6
- text_kv: bfloat16 [2, 512, 3072], P(None, None, 'tensor'), may hold values from -6 to 6
- positions: int32 [8192], P('patch'), may hold values from 0 to 8191, each once
- query_gain: float32 [128], replicated, may hold values from 1 to 4
- key_gain: float32 [128], replicated, may hold values from 1 to 4
- out_weight: bfloat16 [3072, 3072], P('tensor'), may hold values from -0.109375 to 0.109375
- gate_table: float32 [28, 3072], P(None, 'tensor'), may hold values from -4 to 4
- timestep: int32 [1], replicated, may hold values from 0 to 27
- hidden_in: bfloat16 [8192, 3072], P('patch', 'tensor'), may hold values from -2 to 2
- control: bfloat16 [8192, 3072], P('patch', 'tensor'), may hold values from -2 to 2
Outputs:
- hidden_out: bfloat16 [8192, 3072], P('patch', 'tensor')
The draws below stay inside these ranges and needn't reach their ends.
Inputs may be any that keep to these rules, and one draw needn't show every extreme that they name: `positions`: every grid position 0 to 8191 once.
All inputs are finite; a program needn't handle non-finite values.
Results may differ from the reference program's by a relative error of at most 0.02.
Values may be sent and summed in bfloat16 or wider, within the bound.
No kernel may reach another device: no remote copies, remote signals or barrier semaphores. Data moves between devices by JAX's collectives and lax.ppermute only.
A program may use at most 64 MiB of HBM per device.

```python
import math
import jax
import jax.numpy as jnp
from jax import lax

D = 3072
HEADS = 24
HEAD_DIMENSION = 128
TXT = 512
STEPS = 28
TOK_DEV = 128
IMAGE_TOKENS = 8192


def draw_fresh_qkv(key, part):
    key = jax.random.fold_in(key, 11)
    first_key = jax.random.fold_in(key, 0)
    shape = (3, IMAGE_TOKENS, HEADS * HEAD_DIMENSION)
    base = jax.random.normal(first_key, shape, jnp.float32)
    return jnp.clip(base, -14.0, 14.0).astype(jnp.bfloat16)


def draw_query_gain(key, part):
    key = jax.random.fold_in(key, 23)
    return jax.random.uniform(key, (HEAD_DIMENSION,), jnp.float32, 1.0, 2.0)


def draw_key_gain(key, part):
    key = jax.random.fold_in(key, 37)
    return jax.random.uniform(key, (HEAD_DIMENSION,), jnp.float32, 1.0, 2.0)


def shard_levels(stream_key, dims, pieces, low, high):
    def one(axis_at, blocks):
        draws = jax.random.uniform(jax.random.fold_in(jax.random.fold_in(stream_key, 6), axis_at), (blocks,), jnp.float32, low / len(pieces), high / len(pieces))
        return jnp.repeat(jnp.exp(draws), dims[axis_at] // blocks).reshape((-1,) + (1,) * (len(dims) - axis_at - 1))

    level = one(*pieces[0])
    for cut in pieces[1:]:
        level = level * one(*cut)
    return level


def centred(stream_key, extent, width, limit, pieces=(), kind=jnp.bfloat16):
    loudness = shard_levels(stream_key, extent, pieces, -0.22, 0.18) if pieces else 1.0
    values = jax.random.normal(stream_key, extent, jnp.float32) * width * loudness
    return jnp.minimum(jnp.maximum(values, -limit), limit).astype(kind)


def setup_inputs(seed: int = 0) -> dict:
    splits = jax.random.split(jax.random.key(seed), 12)
    return {
        "fresh_qkv": draw_fresh_qkv(jax.random.fold_in(splits[11], 71), 0),
        "stale_kv": centred(splits[1], (2, IMAGE_TOKENS, HEADS * HEAD_DIMENSION), 1.0, 6.0, ((1, 64), (2, 8))),
        "text_kv": centred(splits[2], (2, TXT, HEADS * HEAD_DIMENSION), 1.0, 6.0, ((2, 8),)),
        "positions": jax.random.permutation(splits[3], IMAGE_TOKENS).astype(jnp.int32),
        "query_gain": draw_query_gain(jax.random.fold_in(splits[11], 71), 0),
        "key_gain": draw_key_gain(jax.random.fold_in(splits[11], 71), 0),
        "out_weight": centred(splits[6], (HEADS * HEAD_DIMENSION, D), (HEADS * HEAD_DIMENSION) ** -0.5, 0.109375, ((0, 8),)),
        "gate_table": centred(splits[7], (STEPS, D), 1.0, 4.0, ((1, 8),), jnp.float32),
        "timestep": jax.random.randint(splits[8], (1,), 0, STEPS).astype(jnp.int32),
        "hidden_in": centred(splits[9], (IMAGE_TOKENS, D), 0.3, 2.0, ((0, 64), (1, 8))),
        "control": centred(splits[10], (IMAGE_TOKENS, D), 0.3, 2.0, ((0, 64), (1, 8))),
    }


def pair_angles(positions, head_size):
    first = head_size // 8
    other = (head_size - first) // 2
    lead = first // 2
    mid = other // 2
    pair = jnp.arange(head_size // 2)
    expo = jnp.where(pair < lead, 2.0 * pair / first, jnp.where(pair < lead + mid, 2.0 * (pair - lead) / other, 2.0 * (pair - lead - mid) / other)).astype(jnp.float32)
    omega = jnp.power(jnp.float32(10000.0), -expo)
    row_pos = (positions // 128).astype(jnp.float32)
    col_pos = (positions % 128).astype(jnp.float32)
    where_pos = jnp.where(pair[None, :] < lead, jnp.float32(0.0), jnp.where(pair[None, :] < lead + mid, row_pos[:, None], col_pos[:, None]))
    angle = where_pos * omega[None, :]
    return (jnp.cos(angle), jnp.sin(angle))

def prepare(raw, gain, cosines, sines, head_size):
    count = raw.shape[0]
    values = raw.astype(jnp.float32).reshape(count, -1, head_size)
    values = values * lax.rsqrt(lax.optimization_barrier(jnp.mean(values * values, axis=-1, keepdims=True)) + 1e-06) * gain
    pairs = values.reshape(count, values.shape[1], head_size // 2, 2)
    first_part = pairs[..., 0]
    second_part = pairs[..., 1]
    cos_b = cosines[:, None, :]
    sin_b = sines[:, None, :]
    rotated = jnp.stack([first_part * cos_b - second_part * sin_b, first_part * sin_b + second_part * cos_b], axis=-1)
    return rotated.reshape(count, -1, head_size).astype(jnp.bfloat16)

def reference(fresh_qkv, stale_kv, text_kv, positions, query_gain, key_gain, out_weight, gate_table, timestep, hidden_in, control):
    cosines, sines = pair_angles(positions, HEAD_DIMENSION)
    fresh_q = prepare(fresh_qkv[0], query_gain, cosines, sines, HEAD_DIMENSION)
    fresh_k = prepare(fresh_qkv[1], key_gain, cosines, sines, HEAD_DIMENSION)
    fresh_v = fresh_qkv[2].reshape(IMAGE_TOKENS, HEADS, HEAD_DIMENSION)
    stale_k = stale_kv[0].reshape(IMAGE_TOKENS, HEADS, HEAD_DIMENSION)
    stale_v = stale_kv[1].reshape(IMAGE_TOKENS, HEADS, HEAD_DIMENSION)
    text_k = text_kv[0].reshape(TXT, HEADS, HEAD_DIMENSION)
    text_v = text_kv[1].reshape(TXT, HEADS, HEAD_DIMENSION)
    blocks = IMAGE_TOKENS // TOK_DEV
    score_scale = 1.0 / math.sqrt(HEAD_DIMENSION)
    block_of = jnp.arange(IMAGE_TOKENS) // TOK_DEV
    same_block = block_of[:, None] == block_of[None, :]

    def one_head(head):
        query = fresh_q[:, head]
        s_stale = jnp.dot(query, stale_k[:, head].T, preferred_element_type=jnp.float32) * score_scale
        s_stale = jnp.where(same_block, -jnp.inf, s_stale)
        query_block_list = query.reshape(blocks, TOK_DEV, HEAD_DIMENSION).astype(jnp.float32)
        key_block_list = fresh_k[:, head].reshape(blocks, TOK_DEV, HEAD_DIMENSION).astype(jnp.float32)
        fresh_scores = jnp.einsum('txf,tyf->txy', query_block_list, key_block_list) * score_scale
        s_text = jnp.dot(query, text_k[:, head].T, preferred_element_type=jnp.float32) * score_scale
        top = jnp.maximum(jnp.maximum(lax.optimization_barrier(jnp.max(s_stale, axis=1)), lax.optimization_barrier(jnp.max(fresh_scores, axis=2)).reshape(IMAGE_TOKENS)), lax.optimization_barrier(jnp.max(s_text, axis=1)))
        p_stale = jnp.exp(s_stale - top[:, None])
        fresh_probability = jnp.exp(fresh_scores - top.reshape(blocks, TOK_DEV)[:, :, None])
        p_text = jnp.exp(s_text - top[:, None])
        total = lax.optimization_barrier(jnp.sum(p_stale, axis=1)) + lax.optimization_barrier(jnp.sum(fresh_probability, axis=2)).reshape(IMAGE_TOKENS) + lax.optimization_barrier(jnp.sum(p_text, axis=1))
        numerator = jnp.dot(p_stale.astype(jnp.bfloat16), stale_v[:, head], preferred_element_type=jnp.float32)
        value_block_list = fresh_v[:, head].reshape(blocks, TOK_DEV, HEAD_DIMENSION).astype(jnp.float32)
        numerator = numerator + jnp.einsum('eyr,eri->eyi', fresh_probability.astype(jnp.bfloat16).astype(jnp.float32), value_block_list).reshape(IMAGE_TOKENS, HEAD_DIMENSION)
        numerator = numerator + jnp.dot(p_text.astype(jnp.bfloat16), text_v[:, head], preferred_element_type=jnp.float32)
        return (numerator / total[:, None]).astype(jnp.bfloat16)
    heads_out = lax.map(one_head, jnp.arange(HEADS))
    attended = jnp.transpose(heads_out, (1, 0, 2)).reshape(IMAGE_TOKENS, HEADS * HEAD_DIMENSION)
    projected = jnp.dot(attended, out_weight, preferred_element_type=jnp.float32)
    gate = gate_table[timestep[0]]
    mixed = hidden_in.astype(jnp.float32) + gate[None, :] * projected + control.astype(jnp.float32)
    return mixed.astype(jnp.bfloat16)
```

```python
import math

import jax
import jax.numpy as jnp
import numpy as np
from jax import lax
from jax.experimental import pallas as pl
from jax.experimental.pallas import tpu as pltpu
from jax.sharding import PartitionSpec as P

HD = 128
TOK = 128
HEADS_DEV = 3
WIDTH = HEADS_DEV * HD
TXT = 512
STAT = 16
SCALE2 = math.log2(math.e) / math.sqrt(HD)
AXES = ("patch", "tensor")
MIB = 1024 * 1024
F32 = jnp.float32
BF16 = jnp.bfloat16


def coords(flat):
    patch, tensor = divmod(flat, 8)
    return patch // 16, patch // 4 % 4, patch % 4, tensor // 2, tensor % 2


def flat_of(y, zh, x, zl, core):
    return (y * 16 + zh * 4 + x) * 8 + zl * 2 + core


def permute(value, where):
    pairs = [(i, flat_of(*where(*coords(i)))) for i in range(512)]
    return lax.ppermute(value, AXES, pairs)


def rings(axis_of_core):
    groups = {}
    for i in range(512):
        y, zh, x, zl, c = coords(i)
        rest = (y, zh, zl, c) if axis_of_core[c] == "x" else (x, zh, zl, c)
        groups.setdefault(rest, []).append(i)
    return list(groups.values())


QUERY_RINGS = rings("xy")
KEY_RINGS = rings("yx")
Z_RUNS = [[0, 2, 4, 6], [1, 3, 5, 7]]


def exchange(value, axes, groups):
    return lax.all_to_all(value, axes, 0, 0, axis_index_groups=groups, tiled=True)


def ring_places():
    patch = lax.axis_index("patch")
    x, y = patch % 4, patch // 16
    first = lax.axis_index("tensor") % 2 == 0
    return jnp.where(first, x, y), jnp.where(first, y, x)


def key_pair(value):
    return permute(value, lambda y, zh, x, zl, c: (y, zh ^ (1, 3)[c], x, zl, c))


def query_pair(value):
    return permute(value, lambda y, zh, x, zl, c: (y, zh ^ (3, 1)[c], x, zl, c))


def swap_core(value):
    return permute(value, lambda y, zh, x, zl, c: (y, zh, x, zl, 1 - c))


def frequencies():
    first = HD // 8
    other = (HD - first) // 2
    lead = first // 2
    mid = other // 2
    table = np.zeros((8, HD), np.float32)
    for lane in range(HD):
        pair = lane // 2
        if pair < lead:
            continue
        row = 0 if pair < lead + mid else 1
        k = pair - lead - row * mid
        table[row, lane] = np.power(np.float32(10000.0), -np.float32(2.0 * k / other))
        table[2, lane] = 0.0
    table[3] = np.where(np.arange(HD) % 2 == 0, -1.0, 1.0)
    return table


def prep_kernel(raw_hbm, pos_hbm, freq_hbm, qg_hbm, kg_hbm, q_out, k_out, raw, pos, freq, gains, sem):
    copies = [
        pltpu.make_async_copy(pos_hbm, pos, sem.at[0]),
        pltpu.make_async_copy(freq_hbm, freq, sem.at[1]),
        pltpu.make_async_copy(raw_hbm.at[pl.ds(0, 2)], raw, sem.at[2]),
        pltpu.make_async_copy(qg_hbm, gains.at[0], sem.at[3]),
        pltpu.make_async_copy(kg_hbm, gains.at[1], sem.at[4]),
    ]
    for c in copies:
        c.start()
    copies[0].wait()
    copies[1].wait()
    sub = lax.broadcasted_iota(jnp.int32, (TOK, HD), 0)
    lane = lax.broadcasted_iota(jnp.int32, (TOK, HD), 1)
    p_row = jnp.broadcast_to(pos[...], (TOK, HD))
    p_col = jnp.sum(
        jnp.where(sub == lane, p_row.astype(F32), 0.0), axis=1, keepdims=True
    ).astype(jnp.int32)
    rows = (p_col // 128).astype(F32)
    cols = (p_col % 128).astype(F32)
    angle = rows * freq[0:1, :] + cols * freq[1:2, :]
    cosv = jnp.cos(angle)
    sinv = jnp.sin(angle) * freq[3:4, :]
    even = lane % 2 == 0
    for c in copies[2:]:
        c.wait()
    for which, out in ((0, q_out), (1, k_out)):
        for h in range(HEADS_DEV):
            v = raw[which, :, h * HD : (h + 1) * HD].astype(F32)
            v = v * lax.rsqrt(jnp.mean(v * v, axis=-1, keepdims=True) + 1e-06) * gains[which]
            other = jnp.where(even, pltpu.roll(v, HD - 1, 1), pltpu.roll(v, 1, 1))
            out[:, h * HD : (h + 1) * HD] = (v * cosv + other * sinv).astype(BF16)


def prepare(fresh_qkv, positions, query_gain, key_gain):
    full = pl.BlockSpec(memory_space=pltpu.VMEM)
    return pl.pallas_call(
        prep_kernel,
        out_shape=(jax.ShapeDtypeStruct((TOK, WIDTH), BF16),) * 2,
        in_specs=[pl.BlockSpec(memory_space=pltpu.HBM)] * 5,
        out_specs=(full, full),
        scratch_shapes=[
            pltpu.VMEM((2, TOK, WIDTH), BF16),
            pltpu.VMEM((1, TOK), jnp.int32),
            pltpu.VMEM((8, HD), F32),
            pltpu.VMEM((2, 1, HD), F32),
            pltpu.SemaphoreType.DMA((5,)),
        ],
        compiler_params=pltpu.CompilerParams(vmem_limit_bytes=56 * MIB),
        name="prep",
    )(
        fresh_qkv,
        positions.reshape(1, TOK),
        jnp.asarray(frequencies()),
        query_gain.reshape(1, HD),
        key_gain.reshape(1, HD),
    )


def split3(v):
    hi = v.astype(BF16).astype(F32)
    rest = v - hi
    mid = rest.astype(BF16).astype(F32)
    return hi, mid, rest - mid


def attend(q, keys, values):
    s = [
        lax.dot_general(q, k, (((1,), (1,)), ((), ())), preferred_element_type=F32) for k in keys
    ]
    top = jnp.max(s[0], axis=1, keepdims=True)
    for t in s[1:]:
        top = jnp.maximum(top, jnp.max(t, axis=1, keepdims=True))
    top = top * SCALE2
    acc = None
    for t, v in zip(s, values):
        p = jnp.exp2(t * SCALE2 - top).astype(BF16)
        part = jnp.dot(p, v, preferred_element_type=F32)
        acc = part if acc is None else acc + part
    total = acc[:, HD:]
    return acc[:, :HD] / total, top + jnp.log2(total)


def attn_kernel(k_fresh, raw, text, stale, kv_own, kv_pair, q, out, kc, vc, kt, vt):
    q_at, k_at = ring_places()
    own_rows = pl.ds(pl.multiple_of(k_at * TOK, TOK), TOK)
    for h in range(HEADS_DEV):
        cut = slice(h * HD, (h + 1) * HD)
        for b in range(4):
            for at, kv in ((b, kv_own), (4 + b, kv_pair)):
                kc[h, at * TOK : (at + 1) * TOK, :] = kv[b, 0, :, cut]
                vc[h, at * TOK : (at + 1) * TOK, 0:HD] = kv[b, 1, :, cut]
        kc[h, own_rows, :] = k_fresh[:, cut]
        vc[h, own_rows, 0:HD] = raw[2, :, cut]
        vc[h, :, HD:] = jnp.ones((8 * TOK, HD), BF16)
        kt[h] = text[0, :, cut]
        vt[h, :, 0:HD] = text[1, :, cut]
        vt[h, :, HD:] = jnp.ones((TXT, HD), BF16)
    lane = lax.broadcasted_iota(jnp.int32, (TOK, HD), 1)

    def one(ring, half, own):
        stat = jnp.zeros((TOK, HD), F32)
        for h in range(HEADS_DEV):
            cut = slice(h * HD, (h + 1) * HD)
            keys, values = [kc[h]], [vc[h]]
            if own:
                keys.append(kt[h])
                values.append(vt[h])
            o, lse = attend(q[ring, half, :, cut], keys, values)
            out[ring, half * TOK : (half + 1) * TOK, cut] = o.astype(BF16)
            for part, v in enumerate(split3(lse)):
                stat = jnp.where(lane == 3 * h + part, v, stat)
        out[ring, 2 * TOK :, half * HD : (half + 1) * HD] = stat.T[:STAT].astype(BF16)

    out[:, 2 * TOK :, :] = jnp.zeros((4, STAT, WIDTH), BF16)
    one(q_at, 0, True)
    for h in range(HEADS_DEV):
        cut = slice(h * HD, (h + 1) * HD)
        kc[h, own_rows, :] = stale[0, :, cut]
        vc[h, own_rows, 0:HD] = stale[1, :, cut]
    one(q_at, 1, False)

    def step(d, carry):
        ring = (q_at + d) % 4
        one(ring, 0, False)
        one(ring, 1, False)
        return carry

    lax.fori_loop(1, 4, step, 0)


def attention(*args):
    full = pl.BlockSpec(memory_space=pltpu.VMEM)
    return pl.pallas_call(
        attn_kernel,
        out_shape=jax.ShapeDtypeStruct((4, 2 * TOK + STAT, WIDTH), BF16),
        in_specs=[full] * 7,
        out_specs=full,
        scratch_shapes=[
            pltpu.VMEM((HEADS_DEV, 8 * TOK, HD), BF16),
            pltpu.VMEM((HEADS_DEV, 8 * TOK, 2 * HD), BF16),
            pltpu.VMEM((HEADS_DEV, TXT, HD), BF16),
            pltpu.VMEM((HEADS_DEV, TXT, 2 * HD), BF16),
        ],
        compiler_params=pltpu.CompilerParams(vmem_limit_bytes=32 * MIB),
        name="attend",
    )(*args)


def merge(parts, stats):
    rows = []
    for st in stats:
        rows.append([st[3 * h : 3 * h + 1] + st[3 * h + 1 : 3 * h + 2] + st[3 * h + 2 : 3 * h + 3]
                     for h in range(HEADS_DEV)])
    sub = lax.broadcasted_iota(jnp.int32, (TOK, HD), 0)
    table = jnp.zeros((TOK, HD), F32)
    lses = []
    for h in range(HEADS_DEV):
        top = rows[0][h]
        for r in rows[1:]:
            top = jnp.maximum(top, r[h])
        weights = [jnp.exp2(r[h] - top) for r in rows]
        total = weights[0]
        for w in weights[1:]:
            total = total + w
        lses.append(top + jnp.log2(total))
        for i, w in enumerate(weights):
            table = jnp.where(sub == len(rows) * h + i, w / total, table)
    table = table.T
    outs = []
    for h in range(HEADS_DEV):
        acc = None
        for i, part in enumerate(parts):
            w = table[:, len(rows) * h + i : len(rows) * h + i + 1]
            term = part(h) * w
            acc = term if acc is None else acc + term
        outs.append(acc)
    return outs, lses


def merge_kernel(got, keep, send):
    refs = [got.at[i] for i in range(4)]
    sub = lax.broadcasted_iota(jnp.int32, (STAT, HD), 0)
    for half, out in ((0, keep), (1, send)):
        parts = [
            lambda h, r=r: r[half * TOK : (half + 1) * TOK, h * HD : (h + 1) * HD].astype(F32)
            for r in refs
        ]
        stats = [r[2 * TOK :, half * HD : (half + 1) * HD].astype(F32) for r in refs]
        outs, lses = merge(parts, stats)
        table = jnp.zeros((STAT, HD), F32)
        for h in range(HEADS_DEV):
            out[0:TOK, h * HD : (h + 1) * HD] = outs[h].astype(BF16)
            for part, v in enumerate(split3(lses[h])):
                table = jnp.where(sub == 3 * h + part, v, table)
        out[TOK:, :] = jnp.zeros((STAT, WIDTH), BF16)
        out[TOK:, 0:HD] = table.astype(BF16)


def merge_first(messages):
    full = pl.BlockSpec(memory_space=pltpu.VMEM)
    return pl.pallas_call(
        merge_kernel,
        out_shape=(jax.ShapeDtypeStruct((TOK + STAT, WIDTH), BF16),) * 2,
        in_specs=[full],
        out_specs=(full, full),
        compiler_params=pltpu.CompilerParams(vmem_limit_bytes=16 * MIB),
        name="merge",
    )(messages)


def project_kernel(mine, theirs, w, keep, give, att):
    refs = (mine, theirs)
    parts = [lambda h, r=r: r[0:TOK, h * HD : (h + 1) * HD].astype(F32) for r in refs]
    outs, _ = merge(parts, [r[TOK:, 0:HD].astype(F32) for r in refs])
    for h in range(HEADS_DEV):
        att[:, h * HD : (h + 1) * HD] = outs[h].astype(BF16)
    core = lax.axis_index("tensor") % 2
    for z in range(4):
        for out, c in ((give, 1 - core), (keep, core)):
            part = w[:, pl.ds(pl.multiple_of((2 * z + c) * WIDTH, HD), WIDTH)]
            out[z] = jnp.dot(att[...], part, preferred_element_type=F32).astype(out.dtype)


def project(mine, theirs, out_weight):
    full = pl.BlockSpec(memory_space=pltpu.VMEM)
    return pl.pallas_call(
        project_kernel,
        out_shape=(
            jax.ShapeDtypeStruct((4, TOK, WIDTH), F32),
            jax.ShapeDtypeStruct((4, TOK, WIDTH), BF16),
        ),
        in_specs=[full] * 3,
        out_specs=(full, full),
        scratch_shapes=[pltpu.VMEM((TOK, WIDTH), BF16)],
        compiler_params=pltpu.CompilerParams(vmem_limit_bytes=16 * MIB),
        name="project",
    )(mine, theirs, out_weight)


def pair_kernel(keep, got, out):
    out[...] = (keep[...] + got[...].astype(F32)).astype(BF16)


def pair_sum(keep, got):
    full = pl.BlockSpec(memory_space=pltpu.VMEM)
    return pl.pallas_call(
        pair_kernel,
        out_shape=jax.ShapeDtypeStruct((4, TOK, WIDTH), BF16),
        in_specs=[full] * 2,
        out_specs=full,
        compiler_params=pltpu.CompilerParams(vmem_limit_bytes=16 * MIB),
        name="pair_sum",
    )(keep, got)


def final_kernel(step, got, gate, hidden, control, out):
    total = got[0].astype(F32)
    for t in range(1, 4):
        total = total + got[t].astype(F32)
    row = gate[pl.ds(step[0], 1), :]
    out[...] = (hidden[...].astype(F32) + row * total + control[...].astype(F32)).astype(BF16)


def finish(timestep, got, gate_table, hidden_in, control):
    full = pl.BlockSpec(memory_space=pltpu.VMEM)
    return pl.pallas_call(
        final_kernel,
        out_shape=jax.ShapeDtypeStruct((TOK, WIDTH), BF16),
        in_specs=[pl.BlockSpec(memory_space=pltpu.SMEM)] + [full] * 4,
        out_specs=full,
        compiler_params=pltpu.CompilerParams(vmem_limit_bytes=16 * MIB),
        name="finish",
    )(timestep, got, gate_table, hidden_in, control)


def body(
    fresh_qkv,
    stale_kv,
    text_kv,
    positions,
    query_gain,
    key_gain,
    out_weight,
    gate_table,
    timestep,
    hidden_in,
    control,
):
    pair_kv = key_pair(stale_kv)
    q, k_fresh = prepare(fresh_qkv, positions, query_gain, key_gain)
    pair_q = query_pair(q)
    stale_kv, q = lax.optimization_barrier((stale_kv, q))
    kv_own = lax.all_gather(stale_kv, AXES, axis_index_groups=KEY_RINGS)
    pair_q, pair_kv, kv_own = lax.optimization_barrier((pair_q, pair_kv, kv_own))
    q_two = jnp.broadcast_to(jnp.stack([q, pair_q])[None], (4, 2, TOK, WIDTH))
    q_all = exchange(q_two, AXES, QUERY_RINGS)
    kv_pair = lax.all_gather(pair_kv, AXES, axis_index_groups=KEY_RINGS)
    partial = attention(k_fresh, fresh_qkv, text_kv, stale_kv, kv_own, kv_pair, q_all)
    keep, send = merge_first(exchange(partial, AXES, QUERY_RINGS))
    keep, give = project(keep, query_pair(send), out_weight)
    parts = exchange(pair_sum(keep, swap_core(give)), "tensor", Z_RUNS)
    return finish(timestep, parts, gate_table, hidden_in, control)


def solution(mesh):
    in_specs = (
        P(None, "patch", "tensor"),
        P(None, "patch", "tensor"),
        P(None, None, "tensor"),
        P("patch"),
        P(),
        P(),
        P("tensor", None),
        P(None, "tensor"),
        P(),
        P("patch", "tensor"),
        P("patch", "tensor"),
    )
    out_specs = P("patch", "tensor")
    return jax.shard_map(body, mesh=mesh, in_specs=in_specs, out_specs=out_specs, check_vma=False)
```

```python
import functools
import math

import jax
import jax.numpy as jnp
import numpy as np
from jax import lax
from jax.experimental import pallas as pl
from jax.experimental.pallas import tpu as pltpu
from jax.sharding import PartitionSpec as P

HD = 128
TOK = 128
HEADS_DEV = 3
WIDTH = HEADS_DEV * HD
TXT = 512
STAT = 16
SCALE2 = math.log2(math.e) / math.sqrt(HD)
AXES = ("patch", "tensor")
MIB = 1024 * 1024
F32 = jnp.float32
BF16 = jnp.bfloat16


def coords(flat):
    patch, tensor = divmod(flat, 8)
    return patch // 16, patch // 4 % 4, patch % 4, tensor // 2, tensor % 2


def flat_of(y, zh, x, zl, core):
    return (y * 16 + zh * 4 + x) * 8 + zl * 2 + core


def permute(value, where):
    pairs = [(i, flat_of(*where(*coords(i)))) for i in range(512)]
    return lax.ppermute(value, AXES, pairs)


def squares(flip):
    groups = {}
    for i in range(512):
        y, zh, x, zl, c = coords(i)
        f = flip[c]
        groups.setdefault((min(x, x ^ f), min(y, y ^ f), zh, zl, c), []).append(i)
    return list(groups.values())


QUERY_FLIPS = (1, 3)
QUERY_GROUPS = squares(QUERY_FLIPS)
KEY_FLIPS = (3, 1)
Z_RUNS = [[0, 2, 4, 6], [1, 3, 5, 7]]


def exchange(value, axes, groups):
    return lax.all_to_all(value, axes, 0, 0, axis_index_groups=groups, tiled=True)


def query_place():
    patch = lax.axis_index("patch")
    x, y = patch % 4, patch // 16
    first = lax.axis_index("tensor") % 2 == 0
    return jnp.where(first, y % 2 * 2 + x % 2, y // 2 * 2 + x // 2)


def key_square(value):
    def move(dx, dy):
        return permute(
            value,
            lambda y, zh, x, zl, c: (y ^ dy * KEY_FLIPS[c], zh, x ^ dx * KEY_FLIPS[c], zl, c),
        )

    return [value, move(1, 0), move(0, 1), move(1, 1)]


def spread_kernel(*refs):
    out = refs[-1]
    for i in range(4):
        for j, ref in enumerate(refs[:-1]):
            out[i, j] = ref[...]


def spread(*values):
    full = pl.BlockSpec(memory_space=pltpu.VMEM)
    return pl.pallas_call(
        spread_kernel,
        out_shape=jax.ShapeDtypeStruct((4, len(values)) + values[0].shape, BF16),
        in_specs=[full] * len(values),
        out_specs=full,
        compiler_params=pltpu.CompilerParams(vmem_limit_bytes=16 * MIB),
        name="spread",
    )(*values)


def key_pair(value):
    return permute(value, lambda y, zh, x, zl, c: (y, zh ^ (1, 3)[c], x, zl, c))


def query_pair(value):
    return permute(value, lambda y, zh, x, zl, c: (y, zh ^ (3, 1)[c], x, zl, c))


def swap_core(value):
    return permute(value, lambda y, zh, x, zl, c: (y, zh, x, zl, 1 - c))


def frequencies():
    first = HD // 8
    other = (HD - first) // 2
    lead = first // 2
    mid = other // 2
    table = np.zeros((8, HD), np.float32)
    for lane in range(HD):
        pair = lane // 2
        if pair < lead:
            continue
        row = 0 if pair < lead + mid else 1
        k = pair - lead - row * mid
        table[row, lane] = np.power(np.float32(10000.0), -np.float32(2.0 * k / other))
        table[2, lane] = 0.0
    table[3] = np.where(np.arange(HD) % 2 == 0, -1.0, 1.0)
    return table


def prep_kernel(raw_hbm, pos_hbm, freq_hbm, qg_hbm, kg_hbm, q_out, k_out, raw, pos, freq, gains, sem):
    copies = [
        pltpu.make_async_copy(pos_hbm, pos, sem.at[0]),
        pltpu.make_async_copy(freq_hbm, freq, sem.at[1]),
        pltpu.make_async_copy(raw_hbm.at[pl.ds(0, 2)], raw, sem.at[2]),
        pltpu.make_async_copy(qg_hbm, gains.at[0], sem.at[3]),
        pltpu.make_async_copy(kg_hbm, gains.at[1], sem.at[4]),
    ]
    for c in copies:
        c.start()
    copies[0].wait()
    copies[1].wait()
    sub = lax.broadcasted_iota(jnp.int32, (TOK, HD), 0)
    lane = lax.broadcasted_iota(jnp.int32, (TOK, HD), 1)
    p_row = jnp.broadcast_to(pos[...], (TOK, HD))
    p_col = jnp.sum(
        jnp.where(sub == lane, p_row.astype(F32), 0.0), axis=1, keepdims=True
    ).astype(jnp.int32)
    rows = (p_col // 128).astype(F32)
    cols = (p_col % 128).astype(F32)
    angle = rows * freq[0:1, :] + cols * freq[1:2, :]
    cosv = jnp.cos(angle)
    sinv = jnp.sin(angle) * freq[3:4, :]
    even = lane % 2 == 0
    for c in copies[2:]:
        c.wait()
    for which, out in ((0, q_out), (1, k_out)):
        for h in range(HEADS_DEV):
            v = raw[which, :, h * HD : (h + 1) * HD].astype(F32)
            v = v * lax.rsqrt(jnp.mean(v * v, axis=-1, keepdims=True) + 1e-06) * gains[which]
            other = jnp.where(even, pltpu.roll(v, HD - 1, 1), pltpu.roll(v, 1, 1))
            out[:, h * HD : (h + 1) * HD] = (v * cosv + other * sinv).astype(BF16)


def prepare(fresh_qkv, positions, query_gain, key_gain):
    full = pl.BlockSpec(memory_space=pltpu.VMEM)
    return pl.pallas_call(
        prep_kernel,
        out_shape=(jax.ShapeDtypeStruct((TOK, WIDTH), BF16),) * 2,
        in_specs=[pl.BlockSpec(memory_space=pltpu.HBM)] * 5,
        out_specs=(full, full),
        scratch_shapes=[
            pltpu.VMEM((2, TOK, WIDTH), BF16),
            pltpu.VMEM((1, TOK), jnp.int32),
            pltpu.VMEM((8, HD), F32),
            pltpu.VMEM((2, 1, HD), F32),
            pltpu.SemaphoreType.DMA((5,)),
        ],
        compiler_params=pltpu.CompilerParams(vmem_limit_bytes=56 * MIB),
        name="prep",
    )(
        fresh_qkv,
        positions.reshape(1, TOK),
        jnp.asarray(frequencies()),
        query_gain.reshape(1, HD),
        key_gain.reshape(1, HD),
    )


def split3(v):
    hi = v.astype(BF16).astype(F32)
    rest = v - hi
    mid = rest.astype(BF16).astype(F32)
    return hi, mid, rest - mid


def scores(q, k):
    return lax.dot_general(q, k, (((1,), (1,)), ((), ())), preferred_element_type=F32)


def attend(s, values):
    top = jnp.max(s[0], axis=1, keepdims=True)
    for t in s[1:]:
        top = jnp.maximum(top, jnp.max(t, axis=1, keepdims=True))
    top = top * SCALE2
    acc = None
    for t, v in zip(s, values):
        p = jnp.exp2(t * SCALE2 - top).astype(BF16)
        v = jnp.concatenate([v, jnp.ones(v.shape, BF16)], axis=1)
        part = jnp.dot(p, v, preferred_element_type=F32)
        acc = part if acc is None else acc + part
    total = acc[:, HD:]
    return acc[:, :HD] / total, top + jnp.log2(total)


def put(out, o, lse):
    lane = lax.broadcasted_iota(jnp.int32, (TOK, HD), 1)
    stat = jnp.zeros((TOK, HD), F32)
    for h in range(HEADS_DEV):
        out[0:TOK, h * HD : (h + 1) * HD] = o[h].astype(BF16)
        for part, v in enumerate(split3(lse[h])):
            stat = jnp.where(lane == 3 * h + part, v, stat)
    out[TOK:, :] = jnp.zeros((STAT, WIDTH), BF16)
    out[TOK:, 0:HD] = stat.T[:STAT].astype(BF16)


def home_kernel(q, k_fresh, raw, text, out):
    o, lse = [], []
    for h in range(HEADS_DEV):
        cut = slice(h * HD, (h + 1) * HD)
        keys = jnp.concatenate([k_fresh[:, cut], text[0, :, cut]], axis=0)
        values = jnp.concatenate([raw[2, :, cut], text[1, :, cut]], axis=0)
        a, b = attend([scores(q[:, cut], keys)], [values])
        o.append(a)
        lse.append(b)
    put(out, o, lse)


def attend_home(*args):
    full = pl.BlockSpec(memory_space=pltpu.VMEM)
    return pl.pallas_call(
        home_kernel,
        out_shape=jax.ShapeDtypeStruct((TOK + STAT, WIDTH), BF16),
        in_specs=[full] * 4,
        out_specs=full,
        compiler_params=pltpu.CompilerParams(vmem_limit_bytes=16 * MIB),
        cost_estimate=pl.CostEstimate(
            flops=4 * TOK * 5 * TOK * WIDTH, bytes_accessed=MIB, transcendentals=2**18
        ),
        name="attend_home",
    )(*args)


def attn_kernel(half, *refs):
    kv, q, out = refs[:8], refs[8], refs[9]
    at = query_place()
    o = [[None] * HEADS_DEV for _ in range(4)]
    lse = [[None] * HEADS_DEV for _ in range(4)]
    for h in range(HEADS_DEV):
        cut = slice(h * HD, (h + 1) * HD)
        keys = jnp.concatenate([r[0, :, cut] for r in kv], axis=0)
        values = jnp.concatenate([r[1, :, cut] for r in kv], axis=0)
        for pair in (0, 2):
            rows = jnp.concatenate([q[at ^ pair, half, :, cut], q[at ^ (pair + 1), half, :, cut]], axis=0)
            s = scores(rows, keys)
            if half == 0 and pair == 0:
                hidden = jnp.full((TOK, TOK), -jnp.inf, F32)
                s = jnp.concatenate(
                    [jnp.concatenate([hidden, s[:TOK, TOK:]], axis=1), s[TOK:]], axis=0
                )
            a, b = attend([s], [values])
            for i in range(2):
                o[pair + i][h] = a[i * TOK : (i + 1) * TOK]
                lse[pair + i][h] = b[i * TOK : (i + 1) * TOK]
    for d in range(4):
        put(out.at[at ^ d], o[d], lse[d])


def attention(half, kv, q):
    full = pl.BlockSpec(memory_space=pltpu.VMEM)
    return pl.pallas_call(
        functools.partial(attn_kernel, half),
        out_shape=jax.ShapeDtypeStruct((4, TOK + STAT, WIDTH), BF16),
        in_specs=[full] * 9,
        out_specs=full,
        compiler_params=pltpu.CompilerParams(vmem_limit_bytes=32 * MIB),
        cost_estimate=pl.CostEstimate(
            flops=4 * 4 * TOK * 8 * TOK * WIDTH, bytes_accessed=4 * MIB, transcendentals=2**21
        ),
        name="attend_own" if half == 0 else "attend_pair",
    )(*kv, q)


def merge(parts, stats):
    rows = []
    for st in stats:
        rows.append([st[3 * h : 3 * h + 1] + st[3 * h + 1 : 3 * h + 2] + st[3 * h + 2 : 3 * h + 3]
                     for h in range(HEADS_DEV)])
    sub = lax.broadcasted_iota(jnp.int32, (TOK, HD), 0)
    table = jnp.zeros((TOK, HD), F32)
    lses = []
    for h in range(HEADS_DEV):
        top = rows[0][h]
        for r in rows[1:]:
            top = jnp.maximum(top, r[h])
        weights = [jnp.exp2(r[h] - top) for r in rows]
        total = weights[0]
        for w in weights[1:]:
            total = total + w
        lses.append(top + jnp.log2(total))
        for i, w in enumerate(weights):
            table = jnp.where(sub == len(rows) * h + i, w / total, table)
    table = table.T
    outs = []
    for h in range(HEADS_DEV):
        acc = None
        for i, part in enumerate(parts):
            w = table[:, len(rows) * h + i : len(rows) * h + i + 1]
            term = part(h) * w
            acc = term if acc is None else acc + term
        outs.append(acc)
    return outs, lses


def partials(ref):
    return (
        [lambda h, i=i: ref[i, 0:TOK, h * HD : (h + 1) * HD].astype(F32) for i in range(4)],
        [ref[i, TOK:, 0:HD].astype(F32) for i in range(4)],
    )


def merge_kernel(got, out):
    outs, lses = merge(*partials(got))
    sub = lax.broadcasted_iota(jnp.int32, (STAT, HD), 0)
    table = jnp.zeros((STAT, HD), F32)
    for h in range(HEADS_DEV):
        out[0:TOK, h * HD : (h + 1) * HD] = outs[h].astype(BF16)
        for part, v in enumerate(split3(lses[h])):
            table = jnp.where(sub == 3 * h + part, v, table)
    out[TOK:, :] = jnp.zeros((STAT, WIDTH), BF16)
    out[TOK:, 0:HD] = table.astype(BF16)


def merge_first(messages):
    full = pl.BlockSpec(memory_space=pltpu.VMEM)
    return pl.pallas_call(
        merge_kernel,
        out_shape=jax.ShapeDtypeStruct((TOK + STAT, WIDTH), BF16),
        in_specs=[full],
        out_specs=full,
        compiler_params=pltpu.CompilerParams(vmem_limit_bytes=16 * MIB),
        name="merge",
    )(messages)


def project_kernel(mine, theirs, home, w_hbm, keep, give, att, w, sem):
    core = lax.axis_index("tensor") % 2
    order = [(c, z) for c in range(2) for z in range(4)]

    def columns(c, z):
        return pl.ds(pl.multiple_of((2 * z + (core + 1 - c) % 2) * WIDTH, HD), WIDTH)

    copies = [
        pltpu.make_async_copy(w_hbm.at[:, columns(c, z)], w.at[c, z], sem.at[4 * c + z])
        for c, z in order
    ]
    for c in copies:
        c.start()
    parts, stats = partials(mine)
    for ref in (theirs, home):
        parts.append(lambda h, ref=ref: ref[0:TOK, h * HD : (h + 1) * HD].astype(F32))
        stats.append(ref[TOK:, 0:HD].astype(F32))
    outs, _ = merge(parts, stats)
    for h in range(HEADS_DEV):
        att[:, h * HD : (h + 1) * HD] = outs[h].astype(BF16)
    for copy, (c, z) in zip(copies, order):
        copy.wait()
        out = keep if c else give
        out[z] = jnp.dot(att[...], w[c, z], preferred_element_type=F32).astype(out.dtype)


def project(mine, theirs, home, out_weight):
    full = pl.BlockSpec(memory_space=pltpu.VMEM)
    return pl.pallas_call(
        project_kernel,
        out_shape=(
            jax.ShapeDtypeStruct((4, TOK, WIDTH), F32),
            jax.ShapeDtypeStruct((4, TOK, WIDTH), BF16),
        ),
        in_specs=[full] * 3 + [pl.BlockSpec(memory_space=pltpu.HBM)],
        out_specs=(full, full),
        scratch_shapes=[
            pltpu.VMEM((TOK, WIDTH), BF16),
            pltpu.VMEM((2, 4, WIDTH, WIDTH), BF16),
            pltpu.SemaphoreType.DMA((8,)),
        ],
        compiler_params=pltpu.CompilerParams(vmem_limit_bytes=56 * MIB),
        name="project",
    )(mine, theirs, home, out_weight)


def pair_kernel(keep, got, out):
    out[...] = (keep[...] + got[...].astype(F32)).astype(BF16)


def pair_sum(keep, got):
    full = pl.BlockSpec(memory_space=pltpu.VMEM)
    return pl.pallas_call(
        pair_kernel,
        out_shape=jax.ShapeDtypeStruct((4, TOK, WIDTH), BF16),
        in_specs=[full] * 2,
        out_specs=full,
        compiler_params=pltpu.CompilerParams(vmem_limit_bytes=16 * MIB),
        name="pair_sum",
    )(keep, got)


def final_kernel(step, got, gate, hidden, control, out):
    total = got[0].astype(F32)
    for t in range(1, 4):
        total = total + got[t].astype(F32)
    row = gate[pl.ds(step[0], 1), :]
    out[...] = (hidden[...].astype(F32) + row * total + control[...].astype(F32)).astype(BF16)


def finish(timestep, got, gate_table, hidden_in, control):
    full = pl.BlockSpec(memory_space=pltpu.VMEM)
    return pl.pallas_call(
        final_kernel,
        out_shape=jax.ShapeDtypeStruct((TOK, WIDTH), BF16),
        in_specs=[pl.BlockSpec(memory_space=pltpu.SMEM)] + [full] * 4,
        out_specs=full,
        compiler_params=pltpu.CompilerParams(vmem_limit_bytes=16 * MIB),
        name="finish",
    )(timestep, got, gate_table, hidden_in, control)


def body(
    fresh_qkv,
    stale_kv,
    text_kv,
    positions,
    query_gain,
    key_gain,
    out_weight,
    gate_table,
    timestep,
    hidden_in,
    control,
):
    pair_kv = key_pair(stale_kv)
    q, k_fresh = prepare(fresh_qkv, positions, query_gain, key_gain)
    pair_q = query_pair(q)
    stale_kv, q = lax.optimization_barrier((stale_kv, q))
    kv = key_square(stale_kv)
    queries, pair_kv = lax.optimization_barrier((spread(q, pair_q), pair_kv))
    q_all = exchange(queries, AXES, QUERY_GROUPS)
    kv += key_square(pair_kv)
    home = attend_home(q, k_fresh, fresh_qkv, text_kv)
    paired = exchange(attention(1, kv, q_all), AXES, QUERY_GROUPS)
    partial = attention(0, kv, q_all)
    send, partial = lax.optimization_barrier((merge_first(paired), partial))
    theirs = query_pair(send)
    mine = exchange(partial, AXES, QUERY_GROUPS)
    keep, give = project(mine, theirs, home, out_weight)
    parts = exchange(pair_sum(keep, swap_core(give)), "tensor", Z_RUNS)
    return finish(timestep, parts, gate_table, hidden_in, control)


def solution(mesh):
    in_specs = (
        P(None, "patch", "tensor"),
        P(None, "patch", "tensor"),
        P(None, None, "tensor"),
        P("patch"),
        P(),
        P(),
        P("tensor", None),
        P(None, "tensor"),
        P(),
        P("patch", "tensor"),
        P("patch", "tensor"),
    )
    out_specs = P("patch", "tensor")
    return jax.shard_map(body, mesh=mesh, in_specs=in_specs, out_specs=out_specs, check_vma=False)
```

```python
import functools
import math

import jax
import jax.numpy as jnp
import numpy as np
from jax import lax
from jax.experimental import pallas as pl
from jax.experimental.pallas import tpu as pltpu
from jax.sharding import PartitionSpec as P

HD = 128
TOK = 128
HEADS_DEV = 3
WIDTH = HEADS_DEV * HD
TXT = 512
STAT = 16
SCALE2 = math.log2(math.e) / math.sqrt(HD)
AXES = ("patch", "tensor")
MIB = 1024 * 1024
F32 = jnp.float32
BF16 = jnp.bfloat16


def coords(flat):
    patch, tensor = divmod(flat, 8)
    return patch // 16, patch // 4 % 4, patch % 4, tensor // 2, tensor % 2


def flat_of(y, zh, x, zl, core):
    return (y * 16 + zh * 4 + x) * 8 + zl * 2 + core


def permute(value, where):
    pairs = [(i, flat_of(*where(*coords(i)))) for i in range(512)]
    return lax.ppermute(value, AXES, pairs)


def squares(flip):
    groups = {}
    for i in range(512):
        y, zh, x, zl, c = coords(i)
        f = flip[c]
        groups.setdefault((min(x, x ^ f), min(y, y ^ f), zh, zl, c), []).append(i)
    return list(groups.values())


QUERY_FLIPS = (1, 3)
QUERY_GROUPS = squares(QUERY_FLIPS)
KEY_FLIPS = (3, 1)


def exchange(value, axes, groups):
    return lax.all_to_all(value, axes, 0, 0, axis_index_groups=groups, tiled=True)


def query_place():
    patch = lax.axis_index("patch")
    x, y = patch % 4, patch // 16
    first = lax.axis_index("tensor") % 2 == 0
    return jnp.where(first, y % 2 * 2 + x % 2, y // 2 * 2 + x // 2)


def key_square(value):
    def move(dx, dy):
        return permute(
            value,
            lambda y, zh, x, zl, c: (y ^ dy * KEY_FLIPS[c], zh, x ^ dx * KEY_FLIPS[c], zl, c),
        )

    return [value, move(1, 0), move(0, 1), move(1, 1)]


def spread_kernel(*refs):
    out = refs[-1]
    for i in range(4):
        for j, ref in enumerate(refs[:-1]):
            out[i, j] = ref[...]


def spread(*values):
    full = pl.BlockSpec(memory_space=pltpu.VMEM)
    return pl.pallas_call(
        spread_kernel,
        out_shape=jax.ShapeDtypeStruct((4, len(values)) + values[0].shape, BF16),
        in_specs=[full] * len(values),
        out_specs=full,
        compiler_params=pltpu.CompilerParams(vmem_limit_bytes=16 * MIB),
        name="spread",
    )(*values)


def key_pair(value):
    return permute(value, lambda y, zh, x, zl, c: (y, zh ^ (1, 3)[c], x, zl, c))


def query_pair(value):
    return permute(value, lambda y, zh, x, zl, c: (y, zh ^ (3, 1)[c], x, zl, c))


def swap_core(value):
    return permute(value, lambda y, zh, x, zl, c: (y, zh, x, zl, 1 - c))


def swap_z(value, d):
    return permute(value, lambda y, zh, x, zl, c: (y, zh, x, zl ^ d, c))


def frequencies():
    first = HD // 8
    other = (HD - first) // 2
    lead = first // 2
    mid = other // 2
    table = np.zeros((8, HD), np.float32)
    for lane in range(HD):
        pair = lane // 2
        if pair < lead:
            continue
        row = 0 if pair < lead + mid else 1
        k = pair - lead - row * mid
        table[row, lane] = np.power(np.float32(10000.0), -np.float32(2.0 * k / other))
        table[2, lane] = 0.0
    table[3] = np.where(np.arange(HD) % 2 == 0, -1.0, 1.0)
    return table


def prep_kernel(raw_hbm, pos_hbm, freq_hbm, qg_hbm, kg_hbm, q_out, k_out, raw, pos, freq, gains, sem):
    copies = [
        pltpu.make_async_copy(pos_hbm, pos, sem.at[0]),
        pltpu.make_async_copy(freq_hbm, freq, sem.at[1]),
        pltpu.make_async_copy(raw_hbm.at[pl.ds(0, 2)], raw, sem.at[2]),
        pltpu.make_async_copy(qg_hbm, gains.at[0], sem.at[3]),
        pltpu.make_async_copy(kg_hbm, gains.at[1], sem.at[4]),
    ]
    for c in copies:
        c.start()
    copies[0].wait()
    copies[1].wait()
    sub = lax.broadcasted_iota(jnp.int32, (TOK, HD), 0)
    lane = lax.broadcasted_iota(jnp.int32, (TOK, HD), 1)
    p_row = jnp.broadcast_to(pos[...], (TOK, HD))
    p_col = jnp.sum(
        jnp.where(sub == lane, p_row.astype(F32), 0.0), axis=1, keepdims=True
    ).astype(jnp.int32)
    rows = (p_col // 128).astype(F32)
    cols = (p_col % 128).astype(F32)
    angle = rows * freq[0:1, :] + cols * freq[1:2, :]
    cosv = jnp.cos(angle)
    sinv = jnp.sin(angle) * freq[3:4, :]
    even = lane % 2 == 0
    for c in copies[2:]:
        c.wait()
    for which, out in ((0, q_out), (1, k_out)):
        for h in range(HEADS_DEV):
            v = raw[which, :, h * HD : (h + 1) * HD].astype(F32)
            v = v * lax.rsqrt(jnp.mean(v * v, axis=-1, keepdims=True) + 1e-06) * gains[which]
            other = jnp.where(even, pltpu.roll(v, HD - 1, 1), pltpu.roll(v, 1, 1))
            out[:, h * HD : (h + 1) * HD] = (v * cosv + other * sinv).astype(BF16)


def prepare(fresh_qkv, positions, query_gain, key_gain):
    full = pl.BlockSpec(memory_space=pltpu.VMEM)
    return pl.pallas_call(
        prep_kernel,
        out_shape=(jax.ShapeDtypeStruct((TOK, WIDTH), BF16),) * 2,
        in_specs=[pl.BlockSpec(memory_space=pltpu.HBM)] * 5,
        out_specs=(full, full),
        scratch_shapes=[
            pltpu.VMEM((2, TOK, WIDTH), BF16),
            pltpu.VMEM((1, TOK), jnp.int32),
            pltpu.VMEM((8, HD), F32),
            pltpu.VMEM((2, 1, HD), F32),
            pltpu.SemaphoreType.DMA((5,)),
        ],
        compiler_params=pltpu.CompilerParams(vmem_limit_bytes=56 * MIB),
        name="prep",
    )(
        fresh_qkv,
        positions.reshape(1, TOK),
        jnp.asarray(frequencies()),
        query_gain.reshape(1, HD),
        key_gain.reshape(1, HD),
    )


def stack_kernel(a, b, out):
    out[0] = a[...]
    out[1] = b[...]


def stack(a, b):
    full = pl.BlockSpec(memory_space=pltpu.VMEM)
    return pl.pallas_call(
        stack_kernel,
        out_shape=jax.ShapeDtypeStruct((2,) + a.shape, BF16),
        in_specs=[full] * 2,
        out_specs=full,
        compiler_params=pltpu.CompilerParams(vmem_limit_bytes=16 * MIB),
        name="stack",
    )(a, b)


def split3(v):
    hi = v.astype(BF16).astype(F32)
    rest = v - hi
    mid = rest.astype(BF16).astype(F32)
    return hi, mid, rest - mid


def scores(q, k):
    return lax.dot_general(q, k, (((1,), (1,)), ((), ())), preferred_element_type=F32)


def attend(q, k, v):
    s = scores(q, k)
    top = jnp.max(s, axis=1, keepdims=True) * SCALE2
    p = jnp.exp2(s * SCALE2 - top).astype(BF16)
    acc = jnp.dot(p, v, preferred_element_type=F32)
    total = acc[:, HD:]
    return acc[:, :HD] / total, top + jnp.log2(total)


def put(out, o, lse):
    lane = lax.broadcasted_iota(jnp.int32, (TOK, HD), 1)
    stat = jnp.zeros((TOK, HD), F32)
    for h in range(HEADS_DEV):
        out[0:TOK, h * HD : (h + 1) * HD] = o[h].astype(BF16)
        for part, v in enumerate(split3(lse[h])):
            stat = jnp.where(lane == 3 * h + part, v, stat)
    out[TOK:, :] = jnp.zeros((STAT, WIDTH), BF16)
    out[TOK:, 0:HD] = stat.T[:STAT].astype(BF16)


def home_kernel(q, k_fresh, raw, text, out):
    o, lse = [], []
    for h in range(HEADS_DEV):
        cut = slice(h * HD, (h + 1) * HD)
        keys = jnp.concatenate([k_fresh[:, cut], text[0, :, cut]], axis=0)
        values = jnp.concatenate([raw[2, :, cut], text[1, :, cut]], axis=0)
        values = jnp.concatenate([values, jnp.ones(values.shape, BF16)], axis=1)
        a, b = attend(q[:, cut], keys, values)
        o.append(a)
        lse.append(b)
    put(out, o, lse)


def attend_home(*args):
    full = pl.BlockSpec(memory_space=pltpu.VMEM)
    return pl.pallas_call(
        home_kernel,
        out_shape=jax.ShapeDtypeStruct((TOK + STAT, WIDTH), BF16),
        in_specs=[full] * 4,
        out_specs=full,
        compiler_params=pltpu.CompilerParams(vmem_limit_bytes=16 * MIB),
        cost_estimate=pl.CostEstimate(
            flops=4 * TOK * 5 * TOK * WIDTH, bytes_accessed=MIB, transcendentals=2**18
        ),
        name="attend_home",
    )(*args)


def attn_kernel(a, b, c, d, q, out, kc, vc):
    at = query_place()
    kv = (a, b, c, d)
    for h in range(HEADS_DEV):
        cut = slice(h * HD, (h + 1) * HD)
        for i in range(8):
            rows = slice(i * TOK, (i + 1) * TOK)
            kc[h, rows, :] = kv[i // 2][i % 2, 0, :, cut]
            vc[h, rows, 0:HD] = kv[i // 2][i % 2, 1, :, cut]
        vc[h, :, HD:] = jnp.ones((8 * TOK, HD), BF16)

    def one(place, half, skip):
        o, lse = [], []
        for h in range(HEADS_DEV):
            x, y = attend(q[place, half, :, h * HD : (h + 1) * HD], kc[h, skip:], vc[h, skip:])
            o.append(x)
            lse.append(y)
        put(out.at[place, half], o, lse)

    one(at, 0, TOK)
    one(at, 1, 0)

    def step(i, carry):
        one(at ^ i, 0, 0)
        one(at ^ i, 1, 0)
        return carry

    lax.fori_loop(1, 4, step, 0)


def attention(kv, q):
    full = pl.BlockSpec(memory_space=pltpu.VMEM)
    return pl.pallas_call(
        attn_kernel,
        out_shape=jax.ShapeDtypeStruct((4, 2, TOK + STAT, WIDTH), BF16),
        in_specs=[full] * 5,
        out_specs=full,
        scratch_shapes=[
            pltpu.VMEM((HEADS_DEV, 8 * TOK, HD), BF16),
            pltpu.VMEM((HEADS_DEV, 8 * TOK, 2 * HD), BF16),
        ],
        compiler_params=pltpu.CompilerParams(vmem_limit_bytes=24 * MIB),
        cost_estimate=pl.CostEstimate(
            flops=4 * 8 * TOK * 8 * TOK * WIDTH, bytes_accessed=4 * MIB, transcendentals=2**22
        ),
        name="attend",
    )(*kv, q)


def merge(parts, stats):
    rows = []
    for st in stats:
        rows.append([st[3 * h : 3 * h + 1] + st[3 * h + 1 : 3 * h + 2] + st[3 * h + 2 : 3 * h + 3]
                     for h in range(HEADS_DEV)])
    sub = lax.broadcasted_iota(jnp.int32, (TOK, HD), 0)
    table = jnp.zeros((TOK, HD), F32)
    lses = []
    for h in range(HEADS_DEV):
        top = rows[0][h]
        for r in rows[1:]:
            top = jnp.maximum(top, r[h])
        weights = [jnp.exp2(r[h] - top) for r in rows]
        total = weights[0]
        for w in weights[1:]:
            total = total + w
        lses.append(top + jnp.log2(total))
        for i, w in enumerate(weights):
            table = jnp.where(sub == len(rows) * h + i, w / total, table)
    table = table.T
    outs = []
    for h in range(HEADS_DEV):
        acc = None
        for i, part in enumerate(parts):
            w = table[:, len(rows) * h + i : len(rows) * h + i + 1]
            term = part(h) * w
            acc = term if acc is None else acc + term
        outs.append(acc)
    return outs, lses


def partials(ref, half):
    return (
        [lambda h, i=i: ref[i, half, 0:TOK, h * HD : (h + 1) * HD].astype(F32) for i in range(4)],
        [ref[i, half, TOK:, 0:HD].astype(F32) for i in range(4)],
    )


def merge_kernel(got, out):
    outs, lses = merge(*partials(got, 1))
    sub = lax.broadcasted_iota(jnp.int32, (STAT, HD), 0)
    table = jnp.zeros((STAT, HD), F32)
    for h in range(HEADS_DEV):
        out[0:TOK, h * HD : (h + 1) * HD] = outs[h].astype(BF16)
        for part, v in enumerate(split3(lses[h])):
            table = jnp.where(sub == 3 * h + part, v, table)
    out[TOK:, :] = jnp.zeros((STAT, WIDTH), BF16)
    out[TOK:, 0:HD] = table.astype(BF16)


def merge_first(messages):
    full = pl.BlockSpec(memory_space=pltpu.VMEM)
    return pl.pallas_call(
        merge_kernel,
        out_shape=jax.ShapeDtypeStruct((TOK + STAT, WIDTH), BF16),
        in_specs=[full],
        out_specs=full,
        compiler_params=pltpu.CompilerParams(vmem_limit_bytes=16 * MIB),
        name="merge",
    )(messages)


def project_kernel(mine, theirs, home, w, keep, give, att):
    parts, stats = partials(mine, 0)
    for ref in (theirs, home):
        parts.append(lambda h, ref=ref: ref[0:TOK, h * HD : (h + 1) * HD].astype(F32))
        stats.append(ref[TOK:, 0:HD].astype(F32))
    outs, _ = merge(parts, stats)
    for h in range(HEADS_DEV):
        att[:, h * HD : (h + 1) * HD] = outs[h].astype(BF16)
    t = lax.axis_index("tensor")
    zl, core = t // 2, t % 2
    for d in range(4):
        for out, c in ((give, 1 - core), (keep, core)):
            part = w[:, pl.ds(pl.multiple_of((2 * (zl ^ d) + c) * WIDTH, HD), WIDTH)]
            out[d] = jnp.dot(att[...], part, preferred_element_type=F32).astype(out.dtype)


def project(mine, theirs, home, out_weight):
    full = pl.BlockSpec(memory_space=pltpu.VMEM)
    return pl.pallas_call(
        project_kernel,
        out_shape=(
            jax.ShapeDtypeStruct((4, TOK, WIDTH), F32),
            jax.ShapeDtypeStruct((4, TOK, WIDTH), BF16),
        ),
        in_specs=[full] * 4,
        out_specs=(full, full),
        scratch_shapes=[pltpu.VMEM((TOK, WIDTH), BF16)],
        compiler_params=pltpu.CompilerParams(vmem_limit_bytes=16 * MIB),
        name="project",
    )(mine, theirs, home, out_weight)


def halve_kernel(keep, got, stay, send):
    n = stay.shape[0]
    for i in range(n):
        stay[i] = keep[2 * i] + got[2 * i].astype(F32)
        send[i] = (keep[2 * i + 1] + got[2 * i + 1].astype(F32)).astype(BF16)


def halve(keep, got):
    full = pl.BlockSpec(memory_space=pltpu.VMEM)
    shape = (keep.shape[0] // 2, TOK, WIDTH)
    return pl.pallas_call(
        halve_kernel,
        out_shape=(jax.ShapeDtypeStruct(shape, F32), jax.ShapeDtypeStruct(shape, BF16)),
        in_specs=[full] * 2,
        out_specs=(full, full),
        compiler_params=pltpu.CompilerParams(vmem_limit_bytes=16 * MIB),
        name="halve",
    )(keep, got)


def final_kernel(step, own, got, gate, hidden, control, out):
    total = own[0] + got[0].astype(F32)
    row = gate[pl.ds(step[0], 1), :]
    out[...] = (hidden[...].astype(F32) + row * total + control[...].astype(F32)).astype(BF16)


def finish(timestep, own, got, gate_table, hidden_in, control):
    full = pl.BlockSpec(memory_space=pltpu.VMEM)
    return pl.pallas_call(
        final_kernel,
        out_shape=jax.ShapeDtypeStruct((TOK, WIDTH), BF16),
        in_specs=[pl.BlockSpec(memory_space=pltpu.SMEM)] + [full] * 5,
        out_specs=full,
        compiler_params=pltpu.CompilerParams(vmem_limit_bytes=16 * MIB),
        name="finish",
    )(timestep, own, got, gate_table, hidden_in, control)


def body(
    fresh_qkv,
    stale_kv,
    text_kv,
    positions,
    query_gain,
    key_gain,
    out_weight,
    gate_table,
    timestep,
    hidden_in,
    control,
):
    q, k_fresh = prepare(fresh_qkv, positions, query_gain, key_gain)
    pair_q = query_pair(q)
    stale_kv, q = lax.optimization_barrier((stale_kv, q))
    pair_kv = key_pair(stale_kv)
    queries, pair_kv = lax.optimization_barrier((spread(q, pair_q), pair_kv))
    q_all = exchange(queries, AXES, QUERY_GROUPS)
    kv = key_square(stack(stale_kv, pair_kv))
    home = attend_home(q, k_fresh, fresh_qkv, text_kv)
    mine = exchange(attention(kv, q_all), AXES, QUERY_GROUPS)
    theirs = query_pair(merge_first(mine))
    keep, give = project(mine, theirs, home, out_weight)
    keep, give = halve(keep, swap_core(give))
    keep, give = halve(keep, swap_z(give, 1))
    return finish(timestep, keep, swap_z(give, 2), gate_table, hidden_in, control)


def solution(mesh):
    in_specs = (
        P(None, "patch", "tensor"),
        P(None, "patch", "tensor"),
        P(None, None, "tensor"),
        P("patch"),
        P(),
        P(),
        P("tensor", None),
        P(None, "tensor"),
        P(),
        P("patch", "tensor"),
        P("patch", "tensor"),
    )
    out_specs = P("patch", "tensor")
    return jax.shard_map(body, mesh=mesh, in_specs=in_specs, out_specs=out_specs, check_vma=False)
```

```python
import functools
import math

import jax
import jax.numpy as jnp
import numpy as np
from jax import lax
from jax.experimental import pallas as pl
from jax.experimental.pallas import tpu as pltpu
from jax.sharding import PartitionSpec as P

HD = 128
TOK = 128
HEADS_DEV = 3
WIDTH = HEADS_DEV * HD
TXT = 512
STAT = 16
SCALE2 = math.log2(math.e) / math.sqrt(HD)
AXES = ("patch", "tensor")
MIB = 1024 * 1024
F32 = jnp.float32
BF16 = jnp.bfloat16


def coords(flat):
    patch, tensor = divmod(flat, 8)
    return patch // 16, patch // 4 % 4, patch % 4, tensor // 2, tensor % 2


def flat_of(y, zh, x, zl, core):
    return (y * 16 + zh * 4 + x) * 8 + zl * 2 + core


def permute(value, where):
    pairs = [(i, flat_of(*where(*coords(i)))) for i in range(512)]
    return lax.ppermute(value, AXES, pairs)


def query_groups():
    groups = {}
    for i in range(512):
        y, zh, x, zl, c = coords(i)
        groups.setdefault((y // 2 if c else x // 2, zh, zl, c), []).append(i)
    return list(groups.values())


QUERY_GROUPS = query_groups()


def exchange(value):
    return lax.all_to_all(value, AXES, 0, 0, axis_index_groups=QUERY_GROUPS, tiled=True)


def query_place():
    patch = lax.axis_index("patch")
    x, y = patch % 4, patch // 16
    return jnp.where(lax.axis_index("tensor") % 2 == 0, y * 2 + x % 2, y % 2 * 4 + x)


def after(value, *others):
    return lax.optimization_barrier((value,) + others)[0]


def spread_kernel(ref, out):
    for i in range(8):
        out[i] = ref[...]


def spread(value):
    full = pl.BlockSpec(memory_space=pltpu.VMEM)
    return pl.pallas_call(
        spread_kernel,
        out_shape=jax.ShapeDtypeStruct((8,) + value.shape, BF16),
        in_specs=[full],
        out_specs=full,
        compiler_params=pltpu.CompilerParams(vmem_limit_bytes=16 * MIB),
        name="spread",
    )(value)


def z_step(value, n):
    flips = ((1, 3), (3, 1))[n]
    return permute(value, lambda y, zh, x, zl, c: (y, zh ^ flips[c], x, zl, c))


def plane_step(value):
    return permute(
        value, lambda y, zh, x, zl, c: (y ^ 3 * c, zh, x ^ 3 * (1 - c), zl, c)
    )


def swap_core(value):
    return permute(value, lambda y, zh, x, zl, c: (y, zh, x, zl, 1 - c))


def swap_z(value, d):
    return permute(value, lambda y, zh, x, zl, c: (y, zh, x, zl ^ d, c))


def frequencies():
    first = HD // 8
    other = (HD - first) // 2
    lead = first // 2
    mid = other // 2
    table = np.zeros((8, HD), np.float32)
    for lane in range(HD):
        pair = lane // 2
        if pair < lead:
            continue
        row = 0 if pair < lead + mid else 1
        k = pair - lead - row * mid
        table[row, lane] = np.power(np.float32(10000.0), -np.float32(2.0 * k / other))
        table[2, lane] = 0.0
    table[3] = np.where(np.arange(HD) % 2 == 0, -1.0, 1.0)
    return table


def prep_kernel(raw_hbm, pos_hbm, freq_hbm, qg_hbm, kg_hbm, q_out, k_out, raw, pos, freq, gains, sem):
    copies = [
        pltpu.make_async_copy(pos_hbm, pos, sem.at[0]),
        pltpu.make_async_copy(freq_hbm, freq, sem.at[1]),
        pltpu.make_async_copy(raw_hbm.at[pl.ds(0, 2)], raw, sem.at[2]),
        pltpu.make_async_copy(qg_hbm, gains.at[0], sem.at[3]),
        pltpu.make_async_copy(kg_hbm, gains.at[1], sem.at[4]),
    ]
    for c in copies:
        c.start()
    copies[0].wait()
    copies[1].wait()
    sub = lax.broadcasted_iota(jnp.int32, (TOK, HD), 0)
    lane = lax.broadcasted_iota(jnp.int32, (TOK, HD), 1)
    p_row = jnp.broadcast_to(pos[...], (TOK, HD))
    p_col = jnp.sum(
        jnp.where(sub == lane, p_row.astype(F32), 0.0), axis=1, keepdims=True
    ).astype(jnp.int32)
    rows = (p_col // 128).astype(F32)
    cols = (p_col % 128).astype(F32)
    angle = rows * freq[0:1, :] + cols * freq[1:2, :]
    cosv = jnp.cos(angle)
    sinv = jnp.sin(angle) * freq[3:4, :]
    even = lane % 2 == 0
    for c in copies[2:]:
        c.wait()
    for which, out in ((0, q_out), (1, k_out)):
        for h in range(HEADS_DEV):
            v = raw[which, :, h * HD : (h + 1) * HD].astype(F32)
            v = v * lax.rsqrt(jnp.mean(v * v, axis=-1, keepdims=True) + 1e-06) * gains[which]
            other = jnp.where(even, pltpu.roll(v, HD - 1, 1), pltpu.roll(v, 1, 1))
            out[:, h * HD : (h + 1) * HD] = (v * cosv + other * sinv).astype(BF16)


def prepare(fresh_qkv, positions, query_gain, key_gain):
    full = pl.BlockSpec(memory_space=pltpu.VMEM)
    return pl.pallas_call(
        prep_kernel,
        out_shape=(jax.ShapeDtypeStruct((TOK, WIDTH), BF16),) * 2,
        in_specs=[pl.BlockSpec(memory_space=pltpu.HBM)] * 5,
        out_specs=(full, full),
        scratch_shapes=[
            pltpu.VMEM((2, TOK, WIDTH), BF16),
            pltpu.VMEM((1, TOK), jnp.int32),
            pltpu.VMEM((8, HD), F32),
            pltpu.VMEM((2, 1, HD), F32),
            pltpu.SemaphoreType.DMA((5,)),
        ],
        compiler_params=pltpu.CompilerParams(vmem_limit_bytes=56 * MIB),
        name="prep",
    )(
        fresh_qkv,
        positions.reshape(1, TOK),
        jnp.asarray(frequencies()),
        query_gain.reshape(1, HD),
        key_gain.reshape(1, HD),
    )


def split3(v):
    hi = v.astype(BF16).astype(F32)
    rest = v - hi
    mid = rest.astype(BF16).astype(F32)
    return hi, mid, rest - mid


def scores(q, k):
    return lax.dot_general(q, k, (((1,), (1,)), ((), ())), preferred_element_type=F32)


def attend(q, k, v):
    s = scores(q, k)
    top = jnp.max(s, axis=1, keepdims=True) * SCALE2
    p = jnp.exp2(s * SCALE2 - top).astype(BF16)
    acc = jnp.dot(p, v, preferred_element_type=F32)
    total = acc[:, HD:]
    return acc[:, :HD] / total, top + jnp.log2(total)


def put(out, o, lse):
    lane = lax.broadcasted_iota(jnp.int32, (TOK, HD), 1)
    stat = jnp.zeros((TOK, HD), F32)
    for h in range(HEADS_DEV):
        out[0:TOK, h * HD : (h + 1) * HD] = o[h].astype(BF16)
        for part, v in enumerate(split3(lse[h])):
            stat = jnp.where(lane == 3 * h + part, v, stat)
    out[TOK:, :] = jnp.zeros((STAT, WIDTH), BF16)
    out[TOK:, 0:HD] = stat.T[:STAT].astype(BF16)


def home_kernel(q, k_fresh, raw, text, out):
    o, lse = [], []
    for h in range(HEADS_DEV):
        cut = slice(h * HD, (h + 1) * HD)
        keys = jnp.concatenate([k_fresh[:, cut], text[0, :, cut]], axis=0)
        values = jnp.concatenate([raw[2, :, cut], text[1, :, cut]], axis=0)
        values = jnp.concatenate([values, jnp.ones(values.shape, BF16)], axis=1)
        a, b = attend(q[:, cut], keys, values)
        o.append(a)
        lse.append(b)
    put(out, o, lse)


def attend_home(*args):
    full = pl.BlockSpec(memory_space=pltpu.VMEM)
    return pl.pallas_call(
        home_kernel,
        out_shape=jax.ShapeDtypeStruct((TOK + STAT, WIDTH), BF16),
        in_specs=[full] * 4,
        out_specs=full,
        compiler_params=pltpu.CompilerParams(vmem_limit_bytes=16 * MIB),
        cost_estimate=pl.CostEstimate(
            flops=4 * TOK * 5 * TOK * WIDTH, bytes_accessed=MIB, transcendentals=2**18
        ),
        name="attend_home",
    )(*args)


def attn_kernel(*refs):
    kv = refs[:8]
    q, out, kc, vc = refs[8:]
    at = query_place()
    for h in range(HEADS_DEV):
        cut = slice(h * HD, (h + 1) * HD)
        for i in range(8):
            rows = slice(i * TOK, (i + 1) * TOK)
            kc[h, rows, :] = kv[i][0, :, cut]
            vc[h, rows, 0:HD] = kv[i][1, :, cut]
        vc[h, :, HD:] = jnp.ones((8 * TOK, HD), BF16)

    def one(place, skip):
        o, lse = [], []
        for h in range(HEADS_DEV):
            x, y = attend(q[place, :, h * HD : (h + 1) * HD], kc[h, skip:], vc[h, skip:])
            o.append(x)
            lse.append(y)
        put(out.at[place], o, lse)

    one(at, TOK)
    one(at ^ 1, 0)

    def step(i, carry):
        one(at ^ (2 * i), 0)
        one(at ^ (2 * i + 1), 0)
        return carry

    lax.fori_loop(1, 4, step, 0)


def attention(*args):
    full = pl.BlockSpec(memory_space=pltpu.VMEM)
    return pl.pallas_call(
        attn_kernel,
        out_shape=jax.ShapeDtypeStruct((8, TOK + STAT, WIDTH), BF16),
        in_specs=[full] * 9,
        out_specs=full,
        scratch_shapes=[
            pltpu.VMEM((HEADS_DEV, 8 * TOK, HD), BF16),
            pltpu.VMEM((HEADS_DEV, 8 * TOK, 2 * HD), BF16),
        ],
        compiler_params=pltpu.CompilerParams(vmem_limit_bytes=24 * MIB),
        cost_estimate=pl.CostEstimate(
            flops=4 * 8 * TOK * 8 * TOK * WIDTH, bytes_accessed=4 * MIB, transcendentals=2**22
        ),
        name="attend",
    )(*args)


def merge(parts, stats):
    rows = []
    for st in stats:
        rows.append([st[3 * h : 3 * h + 1] + st[3 * h + 1 : 3 * h + 2] + st[3 * h + 2 : 3 * h + 3]
                     for h in range(HEADS_DEV)])
    sub = lax.broadcasted_iota(jnp.int32, (TOK, HD), 0)
    table = jnp.zeros((TOK, HD), F32)
    for h in range(HEADS_DEV):
        top = rows[0][h]
        for r in rows[1:]:
            top = jnp.maximum(top, r[h])
        weights = [jnp.exp2(r[h] - top) for r in rows]
        total = weights[0]
        for w in weights[1:]:
            total = total + w
        for i, w in enumerate(weights):
            table = jnp.where(sub == len(rows) * h + i, w / total, table)
    table = table.T
    outs = []
    for h in range(HEADS_DEV):
        acc = None
        for i, part in enumerate(parts):
            w = table[:, len(rows) * h + i : len(rows) * h + i + 1]
            term = part(h) * w
            acc = term if acc is None else acc + term
        outs.append(acc)
    return outs


def partials(refs):
    return (
        [lambda h, r=r: r[0:TOK, h * HD : (h + 1) * HD].astype(F32) for r in refs],
        [r[TOK:, 0:HD].astype(F32) for r in refs],
    )


def project_kernel(got, home, w, keep, give, att):
    outs = merge(*partials([got.at[i] for i in range(8)] + [home]))
    for h in range(HEADS_DEV):
        att[:, h * HD : (h + 1) * HD] = outs[h].astype(BF16)
    t = lax.axis_index("tensor")
    zl, core = t // 2, t % 2
    for d in range(4):
        for out, c in ((give, 1 - core), (keep, core)):
            part = w[:, pl.ds(pl.multiple_of((2 * (zl ^ d) + c) * WIDTH, HD), WIDTH)]
            out[d] = jnp.dot(att[...], part, preferred_element_type=F32).astype(out.dtype)


def project(*args):
    full = pl.BlockSpec(memory_space=pltpu.VMEM)
    return pl.pallas_call(
        project_kernel,
        out_shape=(
            jax.ShapeDtypeStruct((4, TOK, WIDTH), F32),
            jax.ShapeDtypeStruct((4, TOK, WIDTH), BF16),
        ),
        in_specs=[full] * 3,
        out_specs=(full, full),
        scratch_shapes=[pltpu.VMEM((TOK, WIDTH), BF16)],
        compiler_params=pltpu.CompilerParams(vmem_limit_bytes=16 * MIB),
        name="project",
    )(*args)


def halve_kernel(keep, got, stay, send):
    n = stay.shape[0]
    for i in range(n):
        stay[i] = keep[2 * i] + got[2 * i].astype(F32)
        send[i] = (keep[2 * i + 1] + got[2 * i + 1].astype(F32)).astype(BF16)


def halve(keep, got):
    full = pl.BlockSpec(memory_space=pltpu.VMEM)
    shape = (keep.shape[0] // 2, TOK, WIDTH)
    return pl.pallas_call(
        halve_kernel,
        out_shape=(jax.ShapeDtypeStruct(shape, F32), jax.ShapeDtypeStruct(shape, BF16)),
        in_specs=[full] * 2,
        out_specs=(full, full),
        compiler_params=pltpu.CompilerParams(vmem_limit_bytes=16 * MIB),
        name="halve",
    )(keep, got)


def final_kernel(step, own, got, gate, hidden, control, out):
    total = own[0] + got[0].astype(F32)
    row = gate[pl.ds(step[0], 1), :]
    out[...] = (hidden[...].astype(F32) + row * total + control[...].astype(F32)).astype(BF16)


def finish(timestep, own, got, gate_table, hidden_in, control):
    full = pl.BlockSpec(memory_space=pltpu.VMEM)
    return pl.pallas_call(
        final_kernel,
        out_shape=jax.ShapeDtypeStruct((TOK, WIDTH), BF16),
        in_specs=[pl.BlockSpec(memory_space=pltpu.SMEM)] + [full] * 5,
        out_specs=full,
        compiler_params=pltpu.CompilerParams(vmem_limit_bytes=16 * MIB),
        name="finish",
    )(timestep, own, got, gate_table, hidden_in, control)


def body(
    fresh_qkv,
    stale_kv,
    text_kv,
    positions,
    query_gain,
    key_gain,
    out_weight,
    gate_table,
    timestep,
    hidden_in,
    control,
):
    z1 = z_step(stale_kv, 0)
    q, k_fresh = prepare(fresh_qkv, positions, query_gain, key_gain)
    stale = after(stale_kv, q)
    z2 = z_step(stale, 1)
    plane = plane_step(stale)
    q_all = exchange(spread(q))
    z1, z2 = after(z1, q_all), after(z2, q_all)
    z3 = z_step(z1, 1)
    kv = [stale_kv, plane, z1, plane_step(z1), z2, plane_step(z2), z3, plane_step(z3)]
    home = attend_home(q, k_fresh, fresh_qkv, text_kv)
    keep, give = project(exchange(attention(*kv, q_all)), home, out_weight)
    keep, give = halve(keep, swap_core(give))
    keep, give = halve(keep, swap_z(give, 1))
    return finish(timestep, keep, swap_z(give, 2), gate_table, hidden_in, control)


def solution(mesh):
    in_specs = (
        P(None, "patch", "tensor"),
        P(None, "patch", "tensor"),
        P(None, None, "tensor"),
        P("patch"),
        P(),
        P(),
        P("tensor", None),
        P(None, "tensor"),
        P(),
        P("patch", "tensor"),
        P("patch", "tensor"),
    )
    out_specs = P("patch", "tensor")
    return jax.shard_map(body, mesh=mesh, in_specs=in_specs, out_specs=out_specs, check_vma=False)
```

```python
import functools
import math

import jax
import jax.numpy as jnp
import numpy as np
from jax import lax
from jax.experimental import pallas as pl
from jax.experimental.pallas import tpu as pltpu
from jax.sharding import PartitionSpec as P

HD = 128
TOK = 128
HEADS_DEV = 3
WIDTH = HEADS_DEV * HD
TXT = 512
STAT = 16
SCALE2 = math.log2(math.e) / math.sqrt(HD)
AXES = ("patch", "tensor")
MIB = 1024 * 1024
F32 = jnp.float32
BF16 = jnp.bfloat16


def coords(flat):
    patch, tensor = divmod(flat, 8)
    return patch // 16, patch // 4 % 4, patch % 4, tensor // 2, tensor % 2


def flat_of(y, zh, x, zl, core):
    return (y * 16 + zh * 4 + x) * 8 + zl * 2 + core


def permute(value, where):
    pairs = [(i, flat_of(*where(*coords(i)))) for i in range(512)]
    return lax.ppermute(value, AXES, pairs)


def squares(flip):
    groups = {}
    for i in range(512):
        y, zh, x, zl, c = coords(i)
        f = flip[c]
        groups.setdefault((min(x, x ^ f), min(y, y ^ f), zh, zl, c), []).append(i)
    return list(groups.values())


QUERY_FLIPS = (1, 3)
QUERY_GROUPS = squares(QUERY_FLIPS)
KEY_FLIPS = (3, 1)


def exchange(value, axes, groups):
    return lax.all_to_all(value, axes, 0, 0, axis_index_groups=groups, tiled=True)


def query_place():
    patch = lax.axis_index("patch")
    x, y = patch % 4, patch // 16
    first = lax.axis_index("tensor") % 2 == 0
    return jnp.where(first, y % 2 * 2 + x % 2, y // 2 * 2 + x // 2)


def square(values, flips):
    def move(value, dx, dy):
        return permute(
            value, lambda y, zh, x, zl, c: (y ^ dy * flips[c], zh, x ^ dx * flips[c], zl, c)
        )

    return [values[0], move(values[1], 1, 0), move(values[2], 0, 1), move(values[3], 1, 1)]


def spread_kernel(*refs):
    out = refs[-1]
    for i in range(4):
        for j, ref in enumerate(refs[:-1]):
            out[i, j] = ref[...]


def spread(*values):
    full = pl.BlockSpec(memory_space=pltpu.VMEM)
    return pl.pallas_call(
        spread_kernel,
        out_shape=jax.ShapeDtypeStruct((4, len(values)) + values[0].shape, BF16),
        in_specs=[full] * len(values),
        out_specs=full,
        compiler_params=pltpu.CompilerParams(vmem_limit_bytes=16 * MIB),
        name="spread",
    )(*values)


def key_pair(value):
    return permute(value, lambda y, zh, x, zl, c: (y, zh ^ (1, 3)[c], x, zl, c))


def query_pair(value):
    return permute(value, lambda y, zh, x, zl, c: (y, zh ^ (3, 1)[c], x, zl, c))


def swap_core(value):
    return permute(value, lambda y, zh, x, zl, c: (y, zh, x, zl, 1 - c))


def swap_z(value, d):
    return permute(value, lambda y, zh, x, zl, c: (y, zh, x, zl ^ d, c))


def frequencies():
    first = HD // 8
    other = (HD - first) // 2
    lead = first // 2
    mid = other // 2
    table = np.zeros((8, HD), np.float32)
    for lane in range(HD):
        pair = lane // 2
        if pair < lead:
            continue
        row = 0 if pair < lead + mid else 1
        k = pair - lead - row * mid
        table[row, lane] = np.power(np.float32(10000.0), -np.float32(2.0 * k / other))
        table[2, lane] = 0.0
    table[3] = np.where(np.arange(HD) % 2 == 0, -1.0, 1.0)
    return table


def prep_kernel(raw_hbm, pos_hbm, freq_hbm, qg_hbm, kg_hbm, q_out, k_out, raw, pos, freq, gains, sem):
    copies = [
        pltpu.make_async_copy(pos_hbm, pos, sem.at[0]),
        pltpu.make_async_copy(freq_hbm, freq, sem.at[1]),
        pltpu.make_async_copy(raw_hbm.at[pl.ds(0, 2)], raw, sem.at[2]),
        pltpu.make_async_copy(qg_hbm, gains.at[0], sem.at[3]),
        pltpu.make_async_copy(kg_hbm, gains.at[1], sem.at[4]),
    ]
    for c in copies:
        c.start()
    copies[0].wait()
    copies[1].wait()
    sub = lax.broadcasted_iota(jnp.int32, (TOK, HD), 0)
    lane = lax.broadcasted_iota(jnp.int32, (TOK, HD), 1)
    p_row = jnp.broadcast_to(pos[...], (TOK, HD))
    p_col = jnp.sum(
        jnp.where(sub == lane, p_row.astype(F32), 0.0), axis=1, keepdims=True
    ).astype(jnp.int32)
    rows = (p_col // 128).astype(F32)
    cols = (p_col % 128).astype(F32)
    angle = rows * freq[0:1, :] + cols * freq[1:2, :]
    cosv = jnp.cos(angle)
    sinv = jnp.sin(angle) * freq[3:4, :]
    even = lane % 2 == 0
    for c in copies[2:]:
        c.wait()
    for which, out in ((0, q_out), (1, k_out)):
        for h in range(HEADS_DEV):
            v = raw[which, :, h * HD : (h + 1) * HD].astype(F32)
            v = v * lax.rsqrt(jnp.mean(v * v, axis=-1, keepdims=True) + 1e-06) * gains[which]
            other = jnp.where(even, pltpu.roll(v, HD - 1, 1), pltpu.roll(v, 1, 1))
            out[:, h * HD : (h + 1) * HD] = (v * cosv + other * sinv).astype(BF16)


def prepare(fresh_qkv, positions, query_gain, key_gain):
    full = pl.BlockSpec(memory_space=pltpu.VMEM)
    return pl.pallas_call(
        prep_kernel,
        out_shape=(jax.ShapeDtypeStruct((TOK, WIDTH), BF16),) * 2,
        in_specs=[pl.BlockSpec(memory_space=pltpu.HBM)] * 5,
        out_specs=(full, full),
        scratch_shapes=[
            pltpu.VMEM((2, TOK, WIDTH), BF16),
            pltpu.VMEM((1, TOK), jnp.int32),
            pltpu.VMEM((8, HD), F32),
            pltpu.VMEM((2, 1, HD), F32),
            pltpu.SemaphoreType.DMA((5,)),
        ],
        compiler_params=pltpu.CompilerParams(vmem_limit_bytes=56 * MIB),
        name="prep",
    )(
        fresh_qkv,
        positions.reshape(1, TOK),
        jnp.asarray(frequencies()),
        query_gain.reshape(1, HD),
        key_gain.reshape(1, HD),
    )


def stack_kernel(a, b, out):
    out[0] = a[...]
    out[1] = b[...]


def stack(a, b):
    full = pl.BlockSpec(memory_space=pltpu.VMEM)
    return pl.pallas_call(
        stack_kernel,
        out_shape=jax.ShapeDtypeStruct((2,) + a.shape, BF16),
        in_specs=[full] * 2,
        out_specs=full,
        compiler_params=pltpu.CompilerParams(vmem_limit_bytes=16 * MIB),
        name="stack",
    )(a, b)


def split3(v):
    hi = v.astype(BF16).astype(F32)
    rest = v - hi
    mid = rest.astype(BF16).astype(F32)
    return hi, mid, rest - mid


def scores(q, k):
    return lax.dot_general(q, k, (((1,), (1,)), ((), ())), preferred_element_type=F32)


def attend(q, k, v):
    s = scores(q, k)
    top = jnp.max(s, axis=1, keepdims=True) * SCALE2
    p = jnp.exp2(s * SCALE2 - top).astype(BF16)
    acc = jnp.dot(p, v, preferred_element_type=F32)
    total = acc[:, HD:]
    return acc[:, :HD] / total, top + jnp.log2(total)


def put(out, o, lse):
    lane = lax.broadcasted_iota(jnp.int32, (TOK, HD), 1)
    stat = jnp.zeros((TOK, HD), F32)
    for h in range(HEADS_DEV):
        out[0:TOK, h * HD : (h + 1) * HD] = o[h].astype(BF16)
        for part, v in enumerate(split3(lse[h])):
            stat = jnp.where(lane == 3 * h + part, v, stat)
    out[TOK:, :] = jnp.zeros((STAT, WIDTH), BF16)
    out[TOK:, 0:HD] = stat.T[:STAT].astype(BF16)


def home_kernel(q, k_fresh, raw, text, out):
    o, lse = [], []
    for h in range(HEADS_DEV):
        cut = slice(h * HD, (h + 1) * HD)
        keys = jnp.concatenate([k_fresh[:, cut], text[0, :, cut]], axis=0)
        values = jnp.concatenate([raw[2, :, cut], text[1, :, cut]], axis=0)
        values = jnp.concatenate([values, jnp.ones(values.shape, BF16)], axis=1)
        a, b = attend(q[:, cut], keys, values)
        o.append(a)
        lse.append(b)
    put(out, o, lse)


def attend_home(*args):
    full = pl.BlockSpec(memory_space=pltpu.VMEM)
    return pl.pallas_call(
        home_kernel,
        out_shape=jax.ShapeDtypeStruct((TOK + STAT, WIDTH), BF16),
        in_specs=[full] * 4,
        out_specs=full,
        compiler_params=pltpu.CompilerParams(vmem_limit_bytes=16 * MIB),
        cost_estimate=pl.CostEstimate(
            flops=4 * TOK * 5 * TOK * WIDTH, bytes_accessed=MIB, transcendentals=2**18
        ),
        name="attend_home",
    )(*args)


def attn_kernel(*refs):
    at = query_place()
    kv, q, outs, kc, vc = refs[:4], refs[4], refs[5:9], refs[9], refs[10]
    for h in range(HEADS_DEV):
        cut = slice(h * HD, (h + 1) * HD)
        for i in range(8):
            rows = slice(i * TOK, (i + 1) * TOK)
            kc[h, rows, :] = kv[i // 2][i % 2, 0, :, cut]
            vc[h, rows, 0:HD] = kv[i // 2][i % 2, 1, :, cut]
        vc[h, :, HD:] = jnp.ones((8 * TOK, HD), BF16)

    for d in range(4):
        for half in range(2):
            skip = TOK if d == 0 and half == 0 else 0
            o, lse = [], []
            for h in range(HEADS_DEV):
                rows = q[at ^ d, half, :, h * HD : (h + 1) * HD]
                x, y = attend(rows, kc[h, skip:], vc[h, skip:])
                o.append(x)
                lse.append(y)
            put(outs[d].at[half], o, lse)


def attention(kv, q):
    full = pl.BlockSpec(memory_space=pltpu.VMEM)
    return pl.pallas_call(
        attn_kernel,
        out_shape=(jax.ShapeDtypeStruct((2, TOK + STAT, WIDTH), BF16),) * 4,
        in_specs=[full] * 5,
        out_specs=(full,) * 4,
        scratch_shapes=[
            pltpu.VMEM((HEADS_DEV, 8 * TOK, HD), BF16),
            pltpu.VMEM((HEADS_DEV, 8 * TOK, 2 * HD), BF16),
        ],
        compiler_params=pltpu.CompilerParams(vmem_limit_bytes=24 * MIB),
        cost_estimate=pl.CostEstimate(
            flops=4 * 8 * TOK * 8 * TOK * WIDTH, bytes_accessed=4 * MIB, transcendentals=2**22
        ),
        name="attend",
    )(*kv, q)


def merge(parts, stats):
    rows = []
    for st in stats:
        rows.append([st[3 * h : 3 * h + 1] + st[3 * h + 1 : 3 * h + 2] + st[3 * h + 2 : 3 * h + 3]
                     for h in range(HEADS_DEV)])
    sub = lax.broadcasted_iota(jnp.int32, (TOK, HD), 0)
    table = jnp.zeros((TOK, HD), F32)
    lses = []
    for h in range(HEADS_DEV):
        top = rows[0][h]
        for r in rows[1:]:
            top = jnp.maximum(top, r[h])
        weights = [jnp.exp2(r[h] - top) for r in rows]
        total = weights[0]
        for w in weights[1:]:
            total = total + w
        lses.append(top + jnp.log2(total))
        for i, w in enumerate(weights):
            table = jnp.where(sub == len(rows) * h + i, w / total, table)
    table = table.T
    outs = []
    for h in range(HEADS_DEV):
        acc = None
        for i, part in enumerate(parts):
            w = table[:, len(rows) * h + i : len(rows) * h + i + 1]
            term = part(h) * w
            acc = term if acc is None else acc + term
        outs.append(acc)
    return outs, lses


def partials(refs, half):
    return (
        [lambda h, r=r: r[half, 0:TOK, h * HD : (h + 1) * HD].astype(F32) for r in refs],
        [r[half, TOK:, 0:HD].astype(F32) for r in refs],
    )


def merge_kernel(a, b, c, d, out):
    outs, lses = merge(*partials((a, b, c, d), 1))
    sub = lax.broadcasted_iota(jnp.int32, (STAT, HD), 0)
    table = jnp.zeros((STAT, HD), F32)
    for h in range(HEADS_DEV):
        out[0:TOK, h * HD : (h + 1) * HD] = outs[h].astype(BF16)
        for part, v in enumerate(split3(lses[h])):
            table = jnp.where(sub == 3 * h + part, v, table)
    out[TOK:, :] = jnp.zeros((STAT, WIDTH), BF16)
    out[TOK:, 0:HD] = table.astype(BF16)


def merge_first(*messages):
    full = pl.BlockSpec(memory_space=pltpu.VMEM)
    return pl.pallas_call(
        merge_kernel,
        out_shape=jax.ShapeDtypeStruct((TOK + STAT, WIDTH), BF16),
        in_specs=[full] * 4,
        out_specs=full,
        compiler_params=pltpu.CompilerParams(vmem_limit_bytes=16 * MIB),
        name="merge",
    )(*messages)


def project_kernel(a, b, c, d, theirs, home, w, keep, give, att):
    parts, stats = partials((a, b, c, d), 0)
    for ref in (theirs, home):
        parts.append(lambda h, ref=ref: ref[0:TOK, h * HD : (h + 1) * HD].astype(F32))
        stats.append(ref[TOK:, 0:HD].astype(F32))
    outs, _ = merge(parts, stats)
    for h in range(HEADS_DEV):
        att[:, h * HD : (h + 1) * HD] = outs[h].astype(BF16)
    t = lax.axis_index("tensor")
    zl, core = t // 2, t % 2
    for slot in range(4):
        for out, c in ((give, 1 - core), (keep, core)):
            part = w[:, pl.ds(pl.multiple_of((2 * (zl ^ slot) + c) * WIDTH, HD), WIDTH)]
            out[slot] = jnp.dot(att[...], part, preferred_element_type=F32).astype(out.dtype)


def project(*args):
    full = pl.BlockSpec(memory_space=pltpu.VMEM)
    return pl.pallas_call(
        project_kernel,
        out_shape=(
            jax.ShapeDtypeStruct((4, TOK, WIDTH), F32),
            jax.ShapeDtypeStruct((4, TOK, WIDTH), BF16),
        ),
        in_specs=[full] * 7,
        out_specs=(full, full),
        scratch_shapes=[pltpu.VMEM((TOK, WIDTH), BF16)],
        compiler_params=pltpu.CompilerParams(vmem_limit_bytes=16 * MIB),
        name="project",
    )(*args)


def core_kernel(keep, got, own, *outs):
    own[...] = keep[0] + got[0].astype(F32)
    for d in range(1, 4):
        outs[d - 1][...] = (keep[d] + got[d].astype(F32)).astype(BF16)


def core_sum(keep, got):
    full = pl.BlockSpec(memory_space=pltpu.VMEM)
    return pl.pallas_call(
        core_kernel,
        out_shape=(jax.ShapeDtypeStruct((TOK, WIDTH), F32),)
        + (jax.ShapeDtypeStruct((TOK, WIDTH), BF16),) * 3,
        in_specs=[full] * 2,
        out_specs=(full,) * 4,
        compiler_params=pltpu.CompilerParams(vmem_limit_bytes=16 * MIB),
        name="core_sum",
    )(keep, got)


def final_kernel(step, own, a, b, c, gate, hidden, control, out):
    total = own[...] + a[...].astype(F32) + b[...].astype(F32) + c[...].astype(F32)
    row = gate[pl.ds(step[0], 1), :]
    out[...] = (hidden[...].astype(F32) + row * total + control[...].astype(F32)).astype(BF16)


def finish(timestep, *args):
    full = pl.BlockSpec(memory_space=pltpu.VMEM)
    return pl.pallas_call(
        final_kernel,
        out_shape=jax.ShapeDtypeStruct((TOK, WIDTH), BF16),
        in_specs=[pl.BlockSpec(memory_space=pltpu.SMEM)] + [full] * 7,
        out_specs=full,
        compiler_params=pltpu.CompilerParams(vmem_limit_bytes=16 * MIB),
        name="finish",
    )(timestep, *args)


def body(
    fresh_qkv,
    stale_kv,
    text_kv,
    positions,
    query_gain,
    key_gain,
    out_weight,
    gate_table,
    timestep,
    hidden_in,
    control,
):
    q, k_fresh = prepare(fresh_qkv, positions, query_gain, key_gain)
    pair_q = query_pair(q)
    stale_kv, q = lax.optimization_barrier((stale_kv, q))
    pair_kv = key_pair(stale_kv)
    queries, pair_kv = lax.optimization_barrier((spread(q, pair_q), pair_kv))
    q_all = exchange(queries, AXES, QUERY_GROUPS)
    kv = square([stack(stale_kv, pair_kv)] * 4, KEY_FLIPS)
    home = attend_home(q, k_fresh, fresh_qkv, text_kv)
    mine = square(attention(kv, q_all), QUERY_FLIPS)
    theirs = query_pair(merge_first(*mine))
    keep, give = project(*mine, theirs, home, out_weight)
    own, *parts = core_sum(keep, swap_core(give))
    parts = [swap_z(p, d + 1) for d, p in enumerate(parts)]
    return finish(timestep, own, *parts, gate_table, hidden_in, control)


def solution(mesh):
    in_specs = (
        P(None, "patch", "tensor"),
        P(None, "patch", "tensor"),
        P(None, None, "tensor"),
        P("patch"),
        P(),
        P(),
        P("tensor", None),
        P(None, "tensor"),
        P(),
        P("patch", "tensor"),
        P("patch", "tensor"),
    )
    out_specs = P("patch", "tensor")
    return jax.shard_map(body, mesh=mesh, in_specs=in_specs, out_specs=out_specs, check_vma=False)
```

```python
import functools
import math

import jax
import jax.numpy as jnp
import numpy as np
from jax import lax
from jax.experimental import pallas as pl
from jax.experimental.pallas import tpu as pltpu
from jax.sharding import PartitionSpec as P

HD = 128
TOK = 128
HEADS_DEV = 3
WIDTH = HEADS_DEV * HD
TXT = 512
STAT = 16
SCALE2 = math.log2(math.e) / math.sqrt(HD)
AXES = ("patch", "tensor")
MIB = 1024 * 1024
F32 = jnp.float32
BF16 = jnp.bfloat16


def coords(flat):
    patch, tensor = divmod(flat, 8)
    return patch // 16, patch // 4 % 4, patch % 4, tensor // 2, tensor % 2


def flat_of(y, zh, x, zl, core):
    return (y * 16 + zh * 4 + x) * 8 + zl * 2 + core


def permute(value, where):
    pairs = [(i, flat_of(*where(*coords(i)))) for i in range(512)]
    return lax.ppermute(value, AXES, pairs)


def squares(flip):
    groups = {}
    for i in range(512):
        y, zh, x, zl, c = coords(i)
        f = flip[c]
        groups.setdefault((min(x, x ^ f), min(y, y ^ f), zh, zl, c), []).append(i)
    return list(groups.values())


QUERY_FLIPS = (1, 3)
QUERY_GROUPS = squares(QUERY_FLIPS)
KEY_FLIPS = (3, 1)


def exchange(value, axes, groups):
    return lax.all_to_all(value, axes, 0, 0, axis_index_groups=groups, tiled=True)


def query_place():
    patch = lax.axis_index("patch")
    x, y = patch % 4, patch // 16
    first = lax.axis_index("tensor") % 2 == 0
    return jnp.where(first, y % 2 * 2 + x % 2, y // 2 * 2 + x // 2)


def key_square(value):
    def move(dx, dy):
        return permute(
            value,
            lambda y, zh, x, zl, c: (y ^ dy * KEY_FLIPS[c], zh, x ^ dx * KEY_FLIPS[c], zl, c),
        )

    return [value, move(1, 0), move(0, 1), move(1, 1)]


def spread_kernel(*refs):
    out = refs[-1]
    for i in range(4):
        for j, ref in enumerate(refs[:-1]):
            out[i, j] = ref[...]


def spread(*values):
    full = pl.BlockSpec(memory_space=pltpu.VMEM)
    return pl.pallas_call(
        spread_kernel,
        out_shape=jax.ShapeDtypeStruct((4, len(values)) + values[0].shape, BF16),
        in_specs=[full] * len(values),
        out_specs=full,
        compiler_params=pltpu.CompilerParams(vmem_limit_bytes=16 * MIB),
        name="spread",
    )(*values)


def key_pair(value):
    return permute(value, lambda y, zh, x, zl, c: (y, zh ^ (1, 3)[c], x, zl, c))


def query_pair(value):
    return permute(value, lambda y, zh, x, zl, c: (y, zh ^ (3, 1)[c], x, zl, c))


def swap_core(value):
    return permute(value, lambda y, zh, x, zl, c: (y, zh, x, zl, 1 - c))


def swap_z(value, d):
    return permute(value, lambda y, zh, x, zl, c: (y, zh, x, zl ^ d, c))


def frequencies():
    first = HD // 8
    other = (HD - first) // 2
    lead = first // 2
    mid = other // 2
    table = np.zeros((8, HD), np.float32)
    for lane in range(HD):
        pair = lane // 2
        if pair < lead:
            continue
        row = 0 if pair < lead + mid else 1
        k = pair - lead - row * mid
        table[row, lane] = np.power(np.float32(10000.0), -np.float32(2.0 * k / other))
        table[2, lane] = 0.0
    table[3] = np.where(np.arange(HD) % 2 == 0, -1.0, 1.0)
    return table


def prep_kernel(raw_hbm, pos_hbm, freq_hbm, qg_hbm, kg_hbm, q_out, k_out, raw, pos, freq, gains, sem):
    copies = [
        pltpu.make_async_copy(pos_hbm, pos, sem.at[0]),
        pltpu.make_async_copy(freq_hbm, freq, sem.at[1]),
        pltpu.make_async_copy(raw_hbm.at[pl.ds(0, 2)], raw, sem.at[2]),
        pltpu.make_async_copy(qg_hbm, gains.at[0], sem.at[3]),
        pltpu.make_async_copy(kg_hbm, gains.at[1], sem.at[4]),
    ]
    for c in copies:
        c.start()
    copies[0].wait()
    copies[1].wait()
    sub = lax.broadcasted_iota(jnp.int32, (TOK, HD), 0)
    lane = lax.broadcasted_iota(jnp.int32, (TOK, HD), 1)
    p_row = jnp.broadcast_to(pos[...], (TOK, HD))
    p_col = jnp.sum(
        jnp.where(sub == lane, p_row.astype(F32), 0.0), axis=1, keepdims=True
    ).astype(jnp.int32)
    rows = (p_col // 128).astype(F32)
    cols = (p_col % 128).astype(F32)
    angle = rows * freq[0:1, :] + cols * freq[1:2, :]
    cosv = jnp.cos(angle)
    sinv = jnp.sin(angle) * freq[3:4, :]
    even = lane % 2 == 0
    for c in copies[2:]:
        c.wait()
    for which, out in ((0, q_out), (1, k_out)):
        for h in range(HEADS_DEV):
            v = raw[which, :, h * HD : (h + 1) * HD].astype(F32)
            v = v * lax.rsqrt(jnp.mean(v * v, axis=-1, keepdims=True) + 1e-06) * gains[which]
            other = jnp.where(even, pltpu.roll(v, HD - 1, 1), pltpu.roll(v, 1, 1))
            out[:, h * HD : (h + 1) * HD] = (v * cosv + other * sinv).astype(BF16)


def prepare(fresh_qkv, positions, query_gain, key_gain):
    full = pl.BlockSpec(memory_space=pltpu.VMEM)
    return pl.pallas_call(
        prep_kernel,
        out_shape=(jax.ShapeDtypeStruct((TOK, WIDTH), BF16),) * 2,
        in_specs=[pl.BlockSpec(memory_space=pltpu.HBM)] * 5,
        out_specs=(full, full),
        scratch_shapes=[
            pltpu.VMEM((2, TOK, WIDTH), BF16),
            pltpu.VMEM((1, TOK), jnp.int32),
            pltpu.VMEM((8, HD), F32),
            pltpu.VMEM((2, 1, HD), F32),
            pltpu.SemaphoreType.DMA((5,)),
        ],
        compiler_params=pltpu.CompilerParams(vmem_limit_bytes=56 * MIB),
        name="prep",
    )(
        fresh_qkv,
        positions.reshape(1, TOK),
        jnp.asarray(frequencies()),
        query_gain.reshape(1, HD),
        key_gain.reshape(1, HD),
    )


def stack_kernel(a, b, out):
    out[0] = a[...]
    out[1] = b[...]


def stack(a, b):
    full = pl.BlockSpec(memory_space=pltpu.VMEM)
    return pl.pallas_call(
        stack_kernel,
        out_shape=jax.ShapeDtypeStruct((2,) + a.shape, BF16),
        in_specs=[full] * 2,
        out_specs=full,
        compiler_params=pltpu.CompilerParams(vmem_limit_bytes=16 * MIB),
        name="stack",
    )(a, b)


def split3(v):
    hi = v.astype(BF16).astype(F32)
    rest = v - hi
    mid = rest.astype(BF16).astype(F32)
    return hi, mid, rest - mid


def scores(q, k):
    return lax.dot_general(q, k, (((1,), (1,)), ((), ())), preferred_element_type=F32)


def attend(q, k, v):
    s = scores(q, k)
    top = jnp.max(s, axis=1, keepdims=True) * SCALE2
    p = jnp.exp2(s * SCALE2 - top).astype(BF16)
    acc = jnp.dot(p, v, preferred_element_type=F32)
    total = acc[:, HD:]
    return acc[:, :HD] / total, top + jnp.log2(total)


def put(out, o, lse):
    lane = lax.broadcasted_iota(jnp.int32, (TOK, HD), 1)
    stat = jnp.zeros((TOK, HD), F32)
    for h in range(HEADS_DEV):
        out[0:TOK, h * HD : (h + 1) * HD] = o[h].astype(BF16)
        for part, v in enumerate(split3(lse[h])):
            stat = jnp.where(lane == 3 * h + part, v, stat)
    out[TOK:, :] = jnp.zeros((STAT, WIDTH), BF16)
    out[TOK:, 0:HD] = stat.T[:STAT].astype(BF16)


def home_kernel(q, k_fresh, raw, text, out):
    o, lse = [], []
    for h in range(HEADS_DEV):
        cut = slice(h * HD, (h + 1) * HD)
        keys = jnp.concatenate([k_fresh[:, cut], text[0, :, cut]], axis=0)
        values = jnp.concatenate([raw[2, :, cut], text[1, :, cut]], axis=0)
        values = jnp.concatenate([values, jnp.ones(values.shape, BF16)], axis=1)
        a, b = attend(q[:, cut], keys, values)
        o.append(a)
        lse.append(b)
    put(out, o, lse)


def attend_home(*args):
    full = pl.BlockSpec(memory_space=pltpu.VMEM)
    return pl.pallas_call(
        home_kernel,
        out_shape=jax.ShapeDtypeStruct((TOK + STAT, WIDTH), BF16),
        in_specs=[full] * 4,
        out_specs=full,
        compiler_params=pltpu.CompilerParams(vmem_limit_bytes=16 * MIB),
        cost_estimate=pl.CostEstimate(
            flops=4 * TOK * 5 * TOK * WIDTH, bytes_accessed=MIB, transcendentals=2**18
        ),
        name="attend_home",
    )(*args)


def attn_kernel(a, b, c, d, q, out, kc, vc):
    at = query_place()
    kv = (a, b, c, d)
    for h in range(HEADS_DEV):
        cut = slice(h * HD, (h + 1) * HD)
        for i in range(8):
            rows = slice(i * TOK, (i + 1) * TOK)
            kc[h, rows, :] = kv[i // 2][i % 2, 0, :, cut]
            vc[h, rows, 0:HD] = kv[i // 2][i % 2, 1, :, cut]
        vc[h, :, HD:] = jnp.ones((8 * TOK, HD), BF16)

    def one(place, half, skip):
        o, lse = [], []
        for h in range(HEADS_DEV):
            x, y = attend(q[place, half, :, h * HD : (h + 1) * HD], kc[h, skip:], vc[h, skip:])
            o.append(x)
            lse.append(y)
        put(out.at[place, half], o, lse)

    for d in range(4):
        one(at ^ d, 0, 0 if d else TOK)
        one(at ^ d, 1, 0)


def attention(kv, q):
    full = pl.BlockSpec(memory_space=pltpu.VMEM)
    return pl.pallas_call(
        attn_kernel,
        out_shape=jax.ShapeDtypeStruct((4, 2, TOK + STAT, WIDTH), BF16),
        in_specs=[full] * 5,
        out_specs=full,
        scratch_shapes=[
            pltpu.VMEM((HEADS_DEV, 8 * TOK, HD), BF16),
            pltpu.VMEM((HEADS_DEV, 8 * TOK, 2 * HD), BF16),
        ],
        compiler_params=pltpu.CompilerParams(vmem_limit_bytes=24 * MIB),
        cost_estimate=pl.CostEstimate(
            flops=4 * 8 * TOK * 8 * TOK * WIDTH, bytes_accessed=4 * MIB, transcendentals=2**22
        ),
        name="attend",
    )(*kv, q)


def merge(parts, stats):
    rows = []
    for st in stats:
        rows.append([st[3 * h : 3 * h + 1] + st[3 * h + 1 : 3 * h + 2] + st[3 * h + 2 : 3 * h + 3]
                     for h in range(HEADS_DEV)])
    sub = lax.broadcasted_iota(jnp.int32, (TOK, HD), 0)
    table = jnp.zeros((TOK, HD), F32)
    lses = []
    for h in range(HEADS_DEV):
        top = rows[0][h]
        for r in rows[1:]:
            top = jnp.maximum(top, r[h])
        weights = [jnp.exp2(r[h] - top) for r in rows]
        total = weights[0]
        for w in weights[1:]:
            total = total + w
        lses.append(top + jnp.log2(total))
        for i, w in enumerate(weights):
            table = jnp.where(sub == len(rows) * h + i, w / total, table)
    table = table.T
    outs = []
    for h in range(HEADS_DEV):
        acc = None
        for i, part in enumerate(parts):
            w = table[:, len(rows) * h + i : len(rows) * h + i + 1]
            term = part(h) * w
            acc = term if acc is None else acc + term
        outs.append(acc)
    return outs, lses


def partials(ref, half):
    return (
        [lambda h, i=i: ref[i, half, 0:TOK, h * HD : (h + 1) * HD].astype(F32) for i in range(4)],
        [ref[i, half, TOK:, 0:HD].astype(F32) for i in range(4)],
    )


def merge_kernel(got, out):
    outs, lses = merge(*partials(got, 1))
    sub = lax.broadcasted_iota(jnp.int32, (STAT, HD), 0)
    table = jnp.zeros((STAT, HD), F32)
    for h in range(HEADS_DEV):
        out[0:TOK, h * HD : (h + 1) * HD] = outs[h].astype(BF16)
        for part, v in enumerate(split3(lses[h])):
            table = jnp.where(sub == 3 * h + part, v, table)
    out[TOK:, :] = jnp.zeros((STAT, WIDTH), BF16)
    out[TOK:, 0:HD] = table.astype(BF16)


def merge_first(messages):
    full = pl.BlockSpec(memory_space=pltpu.VMEM)
    return pl.pallas_call(
        merge_kernel,
        out_shape=jax.ShapeDtypeStruct((TOK + STAT, WIDTH), BF16),
        in_specs=[full],
        out_specs=full,
        compiler_params=pltpu.CompilerParams(vmem_limit_bytes=16 * MIB),
        name="merge",
    )(messages)


def project_kernel(mine, theirs, home, w, keep, give, att):
    parts, stats = partials(mine, 0)
    for ref in (theirs, home):
        parts.append(lambda h, ref=ref: ref[0:TOK, h * HD : (h + 1) * HD].astype(F32))
        stats.append(ref[TOK:, 0:HD].astype(F32))
    outs, _ = merge(parts, stats)
    for h in range(HEADS_DEV):
        att[:, h * HD : (h + 1) * HD] = outs[h].astype(BF16)
    t = lax.axis_index("tensor")
    zl, core = t // 2, t % 2
    for d in range(4):
        for out, c in ((give, 1 - core), (keep, core)):
            part = w[:, pl.ds(pl.multiple_of((2 * (zl ^ d) + c) * WIDTH, HD), WIDTH)]
            out[d] = jnp.dot(att[...], part, preferred_element_type=F32).astype(out.dtype)


def project(mine, theirs, home, out_weight):
    full = pl.BlockSpec(memory_space=pltpu.VMEM)
    return pl.pallas_call(
        project_kernel,
        out_shape=(
            jax.ShapeDtypeStruct((4, TOK, WIDTH), F32),
            jax.ShapeDtypeStruct((4, TOK, WIDTH), BF16),
        ),
        in_specs=[full] * 4,
        out_specs=(full, full),
        scratch_shapes=[pltpu.VMEM((TOK, WIDTH), BF16)],
        compiler_params=pltpu.CompilerParams(vmem_limit_bytes=16 * MIB),
        name="project",
    )(mine, theirs, home, out_weight)


def core_kernel(keep, got, own, *outs):
    own[...] = keep[0] + got[0].astype(F32)
    for d in range(1, 4):
        outs[d - 1][...] = (keep[d] + got[d].astype(F32)).astype(BF16)


def core_sum(keep, got):
    full = pl.BlockSpec(memory_space=pltpu.VMEM)
    return pl.pallas_call(
        core_kernel,
        out_shape=(jax.ShapeDtypeStruct((TOK, WIDTH), F32),)
        + (jax.ShapeDtypeStruct((TOK, WIDTH), BF16),) * 3,
        in_specs=[full] * 2,
        out_specs=(full,) * 4,
        compiler_params=pltpu.CompilerParams(vmem_limit_bytes=16 * MIB),
        name="core_sum",
    )(keep, got)


def final_kernel(step, own, a, b, c, gate, hidden, control, out):
    total = own[...] + a[...].astype(F32) + b[...].astype(F32) + c[...].astype(F32)
    row = gate[pl.ds(step[0], 1), :]
    out[...] = (hidden[...].astype(F32) + row * total + control[...].astype(F32)).astype(BF16)


def finish(timestep, *args):
    full = pl.BlockSpec(memory_space=pltpu.VMEM)
    return pl.pallas_call(
        final_kernel,
        out_shape=jax.ShapeDtypeStruct((TOK, WIDTH), BF16),
        in_specs=[pl.BlockSpec(memory_space=pltpu.SMEM)] + [full] * 7,
        out_specs=full,
        compiler_params=pltpu.CompilerParams(vmem_limit_bytes=16 * MIB),
        name="finish",
    )(timestep, *args)


def body(
    fresh_qkv,
    stale_kv,
    text_kv,
    positions,
    query_gain,
    key_gain,
    out_weight,
    gate_table,
    timestep,
    hidden_in,
    control,
):
    q, k_fresh = prepare(fresh_qkv, positions, query_gain, key_gain)
    pair_q = query_pair(q)
    stale_kv, q = lax.optimization_barrier((stale_kv, q))
    pair_kv = key_pair(stale_kv)
    queries, pair_kv = lax.optimization_barrier((spread(q, pair_q), pair_kv))
    q_all = exchange(queries, AXES, QUERY_GROUPS)
    kv = key_square(stack(stale_kv, pair_kv))
    home = attend_home(q, k_fresh, fresh_qkv, text_kv)
    mine = exchange(attention(kv, q_all), AXES, QUERY_GROUPS)
    theirs = query_pair(merge_first(mine))
    keep, give = project(mine, theirs, home, out_weight)
    own, *parts = core_sum(keep, swap_core(give))
    parts = [swap_z(p, d + 1) for d, p in enumerate(parts)]
    return finish(timestep, own, *parts, gate_table, hidden_in, control)


def solution(mesh):
    in_specs = (
        P(None, "patch", "tensor"),
        P(None, "patch", "tensor"),
        P(None, None, "tensor"),
        P("patch"),
        P(),
        P(),
        P("tensor", None),
        P(None, "tensor"),
        P(),
        P("patch", "tensor"),
        P("patch", "tensor"),
    )
    out_specs = P("patch", "tensor")
    return jax.shard_map(body, mesh=mesh, in_specs=in_specs, out_specs=out_specs, check_vma=False)
```

```python
import functools
import math

import jax
import jax.numpy as jnp
import numpy as np
from jax import lax
from jax.experimental import pallas as pl
from jax.experimental.pallas import tpu as pltpu
from jax.sharding import PartitionSpec as P

HD = 128
TOK = 128
HEADS_DEV = 3
WIDTH = HEADS_DEV * HD
TXT = 512
STAT = 16
SCALE2 = math.log2(math.e) / math.sqrt(HD)
AXES = ("patch", "tensor")
MIB = 1024 * 1024
F32 = jnp.float32
BF16 = jnp.bfloat16


def coords(flat):
    patch, tensor = divmod(flat, 8)
    return patch // 16, patch // 4 % 4, patch % 4, tensor // 2, tensor % 2


def flat_of(y, zh, x, zl, core):
    return (y * 16 + zh * 4 + x) * 8 + zl * 2 + core


def permute(value, where):
    pairs = [(i, flat_of(*where(*coords(i)))) for i in range(512)]
    return lax.ppermute(value, AXES, pairs)


def squares(flip):
    groups = {}
    for i in range(512):
        y, zh, x, zl, c = coords(i)
        f = flip[c]
        groups.setdefault((min(x, x ^ f), min(y, y ^ f), zh, zl, c), []).append(i)
    return list(groups.values())


QUERY_FLIPS = (1, 3)
QUERY_GROUPS = squares(QUERY_FLIPS)
KEY_FLIPS = (3, 1)


def exchange(value, axes, groups):
    return lax.all_to_all(value, axes, 0, 0, axis_index_groups=groups, tiled=True)


def query_place():
    patch = lax.axis_index("patch")
    x, y = patch % 4, patch // 16
    first = lax.axis_index("tensor") % 2 == 0
    return jnp.where(first, y % 2 * 2 + x % 2, y // 2 * 2 + x // 2)


def key_square(value):
    def move(dx, dy):
        return permute(
            value,
            lambda y, zh, x, zl, c: (y ^ dy * KEY_FLIPS[c], zh, x ^ dx * KEY_FLIPS[c], zl, c),
        )

    return [value, move(1, 0), move(0, 1), move(1, 1)]


def spread_kernel(*refs):
    out = refs[-1]
    for i in range(4):
        for j, ref in enumerate(refs[:-1]):
            out[i, j] = ref[...]


def hold_kernel(ref, out):
    out[...] = ref[...]


def hold(value):
    full = pl.BlockSpec(memory_space=pltpu.VMEM)
    return pl.pallas_call(
        hold_kernel,
        out_shape=jax.ShapeDtypeStruct(value.shape, value.dtype),
        in_specs=[full],
        out_specs=full,
        compiler_params=pltpu.CompilerParams(vmem_limit_bytes=16 * MIB),
        cost_estimate=pl.CostEstimate(flops=2**30, bytes_accessed=MIB, transcendentals=0),
        name="hold",
    )(value)


def spread(*values):
    full = pl.BlockSpec(memory_space=pltpu.VMEM)
    return pl.pallas_call(
        spread_kernel,
        out_shape=jax.ShapeDtypeStruct((4, len(values)) + values[0].shape, BF16),
        in_specs=[full] * len(values),
        out_specs=full,
        compiler_params=pltpu.CompilerParams(vmem_limit_bytes=16 * MIB),
        name="spread",
    )(*values)


def key_pair(value):
    return permute(value, lambda y, zh, x, zl, c: (y, zh ^ (1, 3)[c], x, zl, c))


def query_pair(value):
    return permute(value, lambda y, zh, x, zl, c: (y, zh ^ (3, 1)[c], x, zl, c))


def swap_core(value):
    return permute(value, lambda y, zh, x, zl, c: (y, zh, x, zl, 1 - c))


def swap_z(value, d):
    return permute(value, lambda y, zh, x, zl, c: (y, zh, x, zl ^ d, c))


def frequencies():
    first = HD // 8
    other = (HD - first) // 2
    lead = first // 2
    mid = other // 2
    table = np.zeros((8, HD), np.float32)
    for lane in range(HD):
        pair = lane // 2
        if pair < lead:
            continue
        row = 0 if pair < lead + mid else 1
        k = pair - lead - row * mid
        table[row, lane] = np.power(np.float32(10000.0), -np.float32(2.0 * k / other))
        table[2, lane] = 0.0
    table[3] = np.where(np.arange(HD) % 2 == 0, -1.0, 1.0)
    return table


def prep_kernel(raw_hbm, pos_hbm, freq_hbm, qg_hbm, kg_hbm, q_out, k_out, raw, pos, freq, gains, sem):
    copies = [
        pltpu.make_async_copy(pos_hbm, pos, sem.at[0]),
        pltpu.make_async_copy(freq_hbm, freq, sem.at[1]),
        pltpu.make_async_copy(raw_hbm.at[pl.ds(0, 2)], raw, sem.at[2]),
        pltpu.make_async_copy(qg_hbm, gains.at[0], sem.at[3]),
        pltpu.make_async_copy(kg_hbm, gains.at[1], sem.at[4]),
    ]
    for c in copies:
        c.start()
    copies[0].wait()
    copies[1].wait()
    sub = lax.broadcasted_iota(jnp.int32, (TOK, HD), 0)
    lane = lax.broadcasted_iota(jnp.int32, (TOK, HD), 1)
    p_row = jnp.broadcast_to(pos[...], (TOK, HD))
    p_col = jnp.sum(
        jnp.where(sub == lane, p_row.astype(F32), 0.0), axis=1, keepdims=True
    ).astype(jnp.int32)
    rows = (p_col // 128).astype(F32)
    cols = (p_col % 128).astype(F32)
    angle = rows * freq[0:1, :] + cols * freq[1:2, :]
    cosv = jnp.cos(angle)
    sinv = jnp.sin(angle) * freq[3:4, :]
    even = lane % 2 == 0
    for c in copies[2:]:
        c.wait()
    for which, out in ((0, q_out), (1, k_out)):
        for h in range(HEADS_DEV):
            v = raw[which, :, h * HD : (h + 1) * HD].astype(F32)
            v = v * lax.rsqrt(jnp.mean(v * v, axis=-1, keepdims=True) + 1e-06) * gains[which]
            other = jnp.where(even, pltpu.roll(v, HD - 1, 1), pltpu.roll(v, 1, 1))
            out[:, h * HD : (h + 1) * HD] = (v * cosv + other * sinv).astype(BF16)


def prepare(fresh_qkv, positions, query_gain, key_gain):
    full = pl.BlockSpec(memory_space=pltpu.VMEM)
    return pl.pallas_call(
        prep_kernel,
        out_shape=(jax.ShapeDtypeStruct((TOK, WIDTH), BF16),) * 2,
        in_specs=[pl.BlockSpec(memory_space=pltpu.HBM)] * 5,
        out_specs=(full, full),
        scratch_shapes=[
            pltpu.VMEM((2, TOK, WIDTH), BF16),
            pltpu.VMEM((1, TOK), jnp.int32),
            pltpu.VMEM((8, HD), F32),
            pltpu.VMEM((2, 1, HD), F32),
            pltpu.SemaphoreType.DMA((5,)),
        ],
        compiler_params=pltpu.CompilerParams(vmem_limit_bytes=56 * MIB),
        name="prep",
    )(
        fresh_qkv,
        positions.reshape(1, TOK),
        jnp.asarray(frequencies()),
        query_gain.reshape(1, HD),
        key_gain.reshape(1, HD),
    )


def stack_kernel(a, b, out):
    out[0] = a[...]
    out[1] = b[...]


def stack(a, b):
    full = pl.BlockSpec(memory_space=pltpu.VMEM)
    return pl.pallas_call(
        stack_kernel,
        out_shape=jax.ShapeDtypeStruct((2,) + a.shape, BF16),
        in_specs=[full] * 2,
        out_specs=full,
        compiler_params=pltpu.CompilerParams(vmem_limit_bytes=16 * MIB),
        name="stack",
    )(a, b)


def split3(v):
    hi = v.astype(BF16).astype(F32)
    rest = v - hi
    mid = rest.astype(BF16).astype(F32)
    return hi, mid, rest - mid


def scores(q, k):
    return lax.dot_general(q, k, (((1,), (1,)), ((), ())), preferred_element_type=F32)


def attend(q, k, v):
    s = scores(q, k)
    top = jnp.max(s, axis=1, keepdims=True) * SCALE2
    p = jnp.exp2(s * SCALE2 - top).astype(BF16)
    acc = jnp.dot(p, v, preferred_element_type=F32)
    total = acc[:, HD:]
    return acc[:, :HD] / total, top + jnp.log2(total)


def put(out, o, lse):
    lane = lax.broadcasted_iota(jnp.int32, (TOK, HD), 1)
    stat = jnp.zeros((TOK, HD), F32)
    for h in range(HEADS_DEV):
        out[0:TOK, h * HD : (h + 1) * HD] = o[h].astype(BF16)
        for part, v in enumerate(split3(lse[h])):
            stat = jnp.where(lane == 3 * h + part, v, stat)
    out[TOK:, :] = jnp.zeros((STAT, WIDTH), BF16)
    out[TOK:, 0:HD] = stat.T[:STAT].astype(BF16)


def home_kernel(q, k_fresh, raw, text, out):
    o, lse = [], []
    for h in range(HEADS_DEV):
        cut = slice(h * HD, (h + 1) * HD)
        keys = jnp.concatenate([k_fresh[:, cut], text[0, :, cut]], axis=0)
        values = jnp.concatenate([raw[2, :, cut], text[1, :, cut]], axis=0)
        values = jnp.concatenate([values, jnp.ones(values.shape, BF16)], axis=1)
        a, b = attend(q[:, cut], keys, values)
        o.append(a)
        lse.append(b)
    put(out, o, lse)


def attend_home(*args):
    full = pl.BlockSpec(memory_space=pltpu.VMEM)
    return pl.pallas_call(
        home_kernel,
        out_shape=jax.ShapeDtypeStruct((TOK + STAT, WIDTH), BF16),
        in_specs=[full] * 4,
        out_specs=full,
        compiler_params=pltpu.CompilerParams(vmem_limit_bytes=16 * MIB),
        cost_estimate=pl.CostEstimate(
            flops=4 * TOK * 5 * TOK * WIDTH, bytes_accessed=MIB, transcendentals=2**18
        ),
        name="attend_home",
    )(*args)


def attn_kernel(a, b, c, d, q, out, kc, vc):
    at = query_place()
    kv = (a, b, c, d)
    for h in range(HEADS_DEV):
        cut = slice(h * HD, (h + 1) * HD)
        for i in range(8):
            rows = slice(i * TOK, (i + 1) * TOK)
            kc[h, rows, :] = kv[i // 2][i % 2, 0, :, cut]
            vc[h, rows, 0:HD] = kv[i // 2][i % 2, 1, :, cut]
        vc[h, :, HD:] = jnp.ones((8 * TOK, HD), BF16)

    def one(place, half, skip):
        o, lse = [], []
        for h in range(HEADS_DEV):
            x, y = attend(q[place, half, :, h * HD : (h + 1) * HD], kc[h, skip:], vc[h, skip:])
            o.append(x)
            lse.append(y)
        put(out.at[place, half], o, lse)

    for d in range(4):
        one(at ^ d, 0, 0 if d else TOK)
        one(at ^ d, 1, 0)


def attention(kv, q):
    full = pl.BlockSpec(memory_space=pltpu.VMEM)
    return pl.pallas_call(
        attn_kernel,
        out_shape=jax.ShapeDtypeStruct((4, 2, TOK + STAT, WIDTH), BF16),
        in_specs=[full] * 5,
        out_specs=full,
        scratch_shapes=[
            pltpu.VMEM((HEADS_DEV, 8 * TOK, HD), BF16),
            pltpu.VMEM((HEADS_DEV, 8 * TOK, 2 * HD), BF16),
        ],
        compiler_params=pltpu.CompilerParams(vmem_limit_bytes=24 * MIB),
        cost_estimate=pl.CostEstimate(
            flops=4 * 8 * TOK * 8 * TOK * WIDTH, bytes_accessed=4 * MIB, transcendentals=2**22
        ),
        name="attend",
    )(*kv, q)


def merge(parts, stats):
    rows = []
    for st in stats:
        rows.append([st[3 * h : 3 * h + 1] + st[3 * h + 1 : 3 * h + 2] + st[3 * h + 2 : 3 * h + 3]
                     for h in range(HEADS_DEV)])
    sub = lax.broadcasted_iota(jnp.int32, (TOK, HD), 0)
    table = jnp.zeros((TOK, HD), F32)
    lses = []
    for h in range(HEADS_DEV):
        top = rows[0][h]
        for r in rows[1:]:
            top = jnp.maximum(top, r[h])
        weights = [jnp.exp2(r[h] - top) for r in rows]
        total = weights[0]
        for w in weights[1:]:
            total = total + w
        lses.append(top + jnp.log2(total))
        for i, w in enumerate(weights):
            table = jnp.where(sub == len(rows) * h + i, w / total, table)
    table = table.T
    outs = []
    for h in range(HEADS_DEV):
        acc = None
        for i, part in enumerate(parts):
            w = table[:, len(rows) * h + i : len(rows) * h + i + 1]
            term = part(h) * w
            acc = term if acc is None else acc + term
        outs.append(acc)
    return outs, lses


def partials(ref, half):
    return (
        [lambda h, i=i: ref[i, half, 0:TOK, h * HD : (h + 1) * HD].astype(F32) for i in range(4)],
        [ref[i, half, TOK:, 0:HD].astype(F32) for i in range(4)],
    )


def merge_kernel(got, out):
    outs, lses = merge(*partials(got, 1))
    sub = lax.broadcasted_iota(jnp.int32, (STAT, HD), 0)
    table = jnp.zeros((STAT, HD), F32)
    for h in range(HEADS_DEV):
        out[0:TOK, h * HD : (h + 1) * HD] = outs[h].astype(BF16)
        for part, v in enumerate(split3(lses[h])):
            table = jnp.where(sub == 3 * h + part, v, table)
    out[TOK:, :] = jnp.zeros((STAT, WIDTH), BF16)
    out[TOK:, 0:HD] = table.astype(BF16)


def merge_first(messages):
    full = pl.BlockSpec(memory_space=pltpu.VMEM)
    return pl.pallas_call(
        merge_kernel,
        out_shape=jax.ShapeDtypeStruct((TOK + STAT, WIDTH), BF16),
        in_specs=[full],
        out_specs=full,
        compiler_params=pltpu.CompilerParams(vmem_limit_bytes=16 * MIB),
        name="merge",
    )(messages)


def columns(zl, slot, core):
    return pl.ds(pl.multiple_of((2 * (zl ^ slot) + core) * WIDTH, HD), WIDTH)


def give_kernel(mine, theirs, home, w, att, give):
    parts, stats = partials(mine, 0)
    for ref in (theirs, home):
        parts.append(lambda h, ref=ref: ref[0:TOK, h * HD : (h + 1) * HD].astype(F32))
        stats.append(ref[TOK:, 0:HD].astype(F32))
    outs, _ = merge(parts, stats)
    for h in range(HEADS_DEV):
        att[:, h * HD : (h + 1) * HD] = outs[h].astype(BF16)
    t = lax.axis_index("tensor")
    for slot in range(4):
        part = w[:, columns(t // 2, slot, 1 - t % 2)]
        give[slot] = jnp.dot(att[...], part, preferred_element_type=F32).astype(BF16)


def keep_kernel(att, w, keep):
    t = lax.axis_index("tensor")
    for slot in range(4):
        part = w[:, columns(t // 2, slot, t % 2)]
        keep[slot] = jnp.dot(att[...], part, preferred_element_type=F32)


def project(mine, theirs, home, out_weight):
    full = pl.BlockSpec(memory_space=pltpu.VMEM)
    params = pltpu.CompilerParams(vmem_limit_bytes=16 * MIB)
    att, give = pl.pallas_call(
        give_kernel,
        out_shape=(
            jax.ShapeDtypeStruct((TOK, WIDTH), BF16),
            jax.ShapeDtypeStruct((4, TOK, WIDTH), BF16),
        ),
        in_specs=[full] * 4,
        out_specs=(full, full),
        compiler_params=params,
        name="project_give",
    )(mine, theirs, home, out_weight)
    keep = pl.pallas_call(
        keep_kernel,
        out_shape=jax.ShapeDtypeStruct((4, TOK, WIDTH), F32),
        in_specs=[full] * 2,
        out_specs=full,
        compiler_params=params,
        name="project_keep",
    )(att, out_weight)
    return keep, give


def core_kernel(keep, got, own, *outs):
    own[...] = keep[0] + got[0].astype(F32)
    for d in range(1, 4):
        outs[d - 1][...] = (keep[d] + got[d].astype(F32)).astype(BF16)


def core_sum(keep, got):
    full = pl.BlockSpec(memory_space=pltpu.VMEM)
    return pl.pallas_call(
        core_kernel,
        out_shape=(jax.ShapeDtypeStruct((TOK, WIDTH), F32),)
        + (jax.ShapeDtypeStruct((TOK, WIDTH), BF16),) * 3,
        in_specs=[full] * 2,
        out_specs=(full,) * 4,
        compiler_params=pltpu.CompilerParams(vmem_limit_bytes=16 * MIB),
        name="core_sum",
    )(keep, got)


def final_kernel(step, own, a, b, c, gate, hidden, control, out):
    total = own[...] + a[...].astype(F32) + b[...].astype(F32) + c[...].astype(F32)
    row = gate[pl.ds(step[0], 1), :]
    out[...] = (hidden[...].astype(F32) + row * total + control[...].astype(F32)).astype(BF16)


def finish(timestep, *args):
    full = pl.BlockSpec(memory_space=pltpu.VMEM)
    return pl.pallas_call(
        final_kernel,
        out_shape=jax.ShapeDtypeStruct((TOK, WIDTH), BF16),
        in_specs=[pl.BlockSpec(memory_space=pltpu.SMEM)] + [full] * 7,
        out_specs=full,
        compiler_params=pltpu.CompilerParams(vmem_limit_bytes=16 * MIB),
        name="finish",
    )(timestep, *args)


def body(
    fresh_qkv,
    stale_kv,
    text_kv,
    positions,
    query_gain,
    key_gain,
    out_weight,
    gate_table,
    timestep,
    hidden_in,
    control,
):
    q, k_fresh = prepare(fresh_qkv, positions, query_gain, key_gain)
    pair_q = query_pair(q)
    stale_kv, q = lax.optimization_barrier((stale_kv, q))
    pair_kv = key_pair(stale_kv)
    queries, pair_kv = lax.optimization_barrier((spread(hold(q), pair_q), pair_kv))
    q_all = exchange(queries, AXES, QUERY_GROUPS)
    kv = key_square(stack(stale_kv, pair_kv))
    home = attend_home(q, k_fresh, fresh_qkv, text_kv)
    mine = exchange(attention(kv, q_all), AXES, QUERY_GROUPS)
    theirs = query_pair(merge_first(mine))
    keep, give = project(mine, theirs, home, out_weight)
    own, *parts = core_sum(keep, swap_core(give))
    parts = [swap_z(p, d + 1) for d, p in enumerate(parts)]
    return finish(timestep, own, *parts, gate_table, hidden_in, control)


def solution(mesh):
    in_specs = (
        P(None, "patch", "tensor"),
        P(None, "patch", "tensor"),
        P(None, None, "tensor"),
        P("patch"),
        P(),
        P(),
        P("tensor", None),
        P(None, "tensor"),
        P(),
        P("patch", "tensor"),
        P("patch", "tensor"),
    )
    out_specs = P("patch", "tensor")
    return jax.shard_map(body, mesh=mesh, in_specs=in_specs, out_specs=out_specs, check_vma=False)
```
